512 devices in a mesh: seq: 64 (over y_lo, z, core), chan: 8 (over x, y_hi).
Axes of the slice: x: 4, y: 8 (y_hi: 2, y_lo: 4; y = y_hi * 4 + y_lo), z: 8, core: 2. Of those that a mesh axis runs over, the one named last changes fastest.
Arguments:
- gate_in: bfloat16 [8192, 4096], P('seq', 'chan'), may hold values from -40 to 40
- key_in: bfloat16 [8192, 4096], P('seq', 'chan'), may hold values from -6 to 6
- value_in: bfloat16 [8192, 4096], P('seq', 'chan'), may hold values from -6 to 6
- out_grad: bfloat16 [8192, 4096], P('seq', 'chan'), may hold values from -6 to 6
- residue: float32 [16, 4096], P(None, 'chan'), may hold values from -4 to 4
- log_rate: float32 [16, 4096], P(None, 'chan'), may hold values from -14 to -3
- skip: float32 [4096], P('chan'), may hold values from -4 to 4
Outputs:
- gated_out: bfloat16 [8192, 4096], P('seq', 'chan')
- gate_grad: bfloat16 [8192, 4096], P('seq', 'chan')
- key_grad: bfloat16 [8192, 4096], P('seq', 'chan')
- value_grad: bfloat16 [8192, 4096], P('seq', 'chan')
- residue_grad: float32 [16, 4096], P(None, 'chan')
- log_rate_grad: float32 [16, 4096], P(None, 'chan')
- skip_grad: float32 [4096], P('chan')
The draws below stay inside these ranges and needn't reach their ends.
All inputs are finite; a program needn't handle non-finite values.
Results may differ from the reference program's by a relative error of at most 0.002.
Values sent between devices are 32-bit elements; how exact they have to be, the bound alone decides.
No kernel may reach another device: no remote copies, remote signals or barrier semaphores. Data moves between devices by JAX's collectives and lax.ppermute only.
A program may use at most 64 MiB of HBM per device.

```python
import math
import jax
import jax.numpy as jnp
from jax import lax

CHANNELS = 4096
MODES = 16
SEQ_LEN = 8192


def draw_gate_in(key, part):
    key = jax.random.fold_in(key, 23)
    base_key = jax.random.fold_in(key, 0)
    base_draw = jax.random.truncated_normal(base_key, -4.0, 4.0, (SEQ_LEN, CHANNELS), jnp.float32)
    column_pos = jnp.arange(CHANNELS, dtype=jnp.float32) / CHANNELS
    scale_field = jnp.exp(column_pos * math.log(3.0))[None, :] * jnp.ones((SEQ_LEN, 1), jnp.float32)
    return (base_draw * scale_field).astype(jnp.bfloat16)


def draw_log_rate(key, part):
    key = jax.random.fold_in(key, 11)
    pick_key, slow_key, fast_key = jax.random.split(key, 3)
    grid_shape = (MODES, CHANNELS)
    lowest = math.log(1.0 / (8.0 * SEQ_LEN))
    middle = math.log(2.0 / SEQ_LEN)
    highest = math.log(1.0 / 30.0)
    slow_share = 0.5
    picker = jax.random.uniform(pick_key, grid_shape, jnp.float32)
    slow_rates = lowest + (middle - lowest) * jax.random.uniform(slow_key, grid_shape, jnp.float32)
    fast_rates = middle + (highest - middle) * jax.random.uniform(fast_key, grid_shape, jnp.float32)
    return jnp.where(picker < slow_share, slow_rates, fast_rates).astype(jnp.float32)


def level_of(key, extent, cuts, low, high):
    gain = 1.0
    for axis_at, blocks in cuts:
        steps = jax.random.uniform(jax.random.fold_in(jax.random.fold_in(key, 6), axis_at), (blocks,), jnp.float32, low / len(cuts), high / len(cuts))
        gain = gain * jnp.repeat(jnp.exp(steps), extent[axis_at] // blocks).reshape((-1,) + (1,) * (len(extent) - 1 - axis_at))
    return gain


def bell_draw(own_key, dims, scale, limit, cuts=(), kind=jnp.bfloat16):
    level = level_of(own_key, dims, cuts, -0.22, 0.18) if cuts else 1.0
    values = jax.random.normal(own_key, dims, jnp.float32) * scale * level
    return jnp.minimum(jnp.maximum(values, -limit), limit).astype(kind)


def setup_inputs(seed: int = 0) -> dict:
    arg_keys = jax.random.split(jax.random.key(seed), 8)
    gate_in = draw_gate_in(jax.random.fold_in(arg_keys[7], 71), 0)
    key_in = bell_draw(arg_keys[1], (SEQ_LEN, CHANNELS), 1.0, 6.0, ((0, 64), (1, 8)))
    value_in = bell_draw(arg_keys[2], (SEQ_LEN, CHANNELS), 1.0, 6.0, ((0, 64), (1, 8)))
    out_grad = bell_draw(arg_keys[3], (SEQ_LEN, CHANNELS), 1.0, 6.0, ((0, 64), (1, 8)))
    residue = bell_draw(arg_keys[4], (MODES, CHANNELS), 1.0, 4.0, ((1, 8),), jnp.float32)
    log_rate = draw_log_rate(jax.random.fold_in(arg_keys[7], 71), 0)
    skip = bell_draw(arg_keys[6], (CHANNELS,), 1.0, 4.0, ((0, 8),), jnp.float32)
    return {"gate_in": gate_in, "key_in": key_in, "value_in": value_in, "out_grad": out_grad, "residue": residue, "log_rate": log_rate, "skip": skip}


CLIP_RMS = 1.0

def layer_block(gate_part, key_part, value_part, res_part, log_part, skip_part):
    length = gate_part.shape[0]
    decay_rate = jnp.exp(log_part)
    amplitude = res_part * jnp.sqrt(2.0 * decay_rate / res_part.shape[0])
    positions = jnp.arange(length, dtype=jnp.float32)
    taps = lax.optimization_barrier(jnp.sum(amplitude[:, None, :] * jnp.exp(-decay_rate[:, None, :] * positions[None, :, None]), axis=0))
    mixed_field = key_part * value_part
    spectrum = jnp.fft.fft(mixed_field, n=2 * length, axis=0) * jnp.fft.fft(taps, n=2 * length, axis=0)
    convolved = jnp.real(jnp.fft.ifft(spectrum, axis=0))[:length]
    return gate_part * (convolved + skip_part * mixed_field)

def reference(gate_in, key_in, value_in, out_grad, residue, log_rate, skip):
    block_width = 128
    blocks = CHANNELS // block_width

    def cut_rows(array):
        return jnp.transpose(array.reshape(array.shape[0], blocks, block_width), (1, 0, 2))

    def join_rows(array):
        return jnp.transpose(array, (1, 0, 2)).reshape(array.shape[1], blocks * block_width)

    def process_block(block_items):
        gate_part, key_part, value_part, grad_part, res_part, log_part, skip_part = block_items
        result, pullback = jax.vjp(layer_block, gate_part.astype(jnp.float32), key_part.astype(jnp.float32), value_part.astype(jnp.float32), res_part, log_part, skip_part)
        d_gate, d_key, d_value, d_res, d_log, d_skip = pullback(grad_part.astype(jnp.float32))
        return (result.astype(jnp.bfloat16), d_gate.astype(jnp.bfloat16), d_key.astype(jnp.bfloat16), d_value.astype(jnp.bfloat16), d_res, d_log, d_skip)
    results = lax.map(process_block, (cut_rows(gate_in), cut_rows(key_in), cut_rows(value_in), cut_rows(out_grad), cut_rows(residue), cut_rows(log_rate), skip.reshape(blocks, block_width)))
    raw_res = join_rows(results[4])
    raw_log = join_rows(results[5])
    raw_skip = results[6].reshape(CHANNELS)
    squares = jnp.sum(raw_res * raw_res) + jnp.sum(raw_log * raw_log) + jnp.sum(raw_skip * raw_skip)
    root_mean = jnp.sqrt(squares / ((2 * MODES + 1) * CHANNELS))
    factor = CLIP_RMS / jnp.maximum(root_mean, CLIP_RMS)
    return (join_rows(results[0]), join_rows(results[1]), join_rows(results[2]), join_rows(results[3]), raw_res * factor, raw_log * factor, raw_skip * factor)
```

```python
import functools

import jax
import jax.numpy as jnp
from jax import lax
from jax.experimental import pallas as pl
from jax.experimental.pallas import tpu as pltpu
from jax.sharding import PartitionSpec as P

CLIP_RMS = 1.0
LANES = 128
SUBLANES = 8
ROWS_OUT = 8
ROWS_BACK = 8
VMEM = pl.BlockSpec(memory_space=pltpu.VMEM)
PARAMS = pltpu.CompilerParams(vmem_limit_bytes=32 * 1024 * 1024)


def tile_of(ref, chunk, group):
    return ref[pl.ds(pl.multiple_of(chunk * SUBLANES, SUBLANES), SUBLANES), group * LANES : (group + 1) * LANES]


def spread(tile, row):
    return jnp.broadcast_to(tile[row : row + 1], (SUBLANES, LANES))


def summary_kernel(key_ref, value_ref, gate_ref, grad_ref, rate_ref, out_ref, mixed, slope):
    block, width = key_ref.shape
    modes = rate_ref.shape[0]
    halves, groups = modes // SUBLANES, width // LANES
    mixed[...] = key_ref[...].astype(jnp.float32) * value_ref[...].astype(jnp.float32)
    slope[...] = grad_ref[...].astype(jnp.float32) * gate_ref[...].astype(jnp.float32)
    steps = {}
    for half in range(halves):
        for group in range(groups):
            rate = jnp.exp(rate_ref[half * SUBLANES : (half + 1) * SUBLANES, group * LANES : (group + 1) * LANES])
            steps[half, group] = jnp.exp(-rate)
    zero = jnp.zeros((SUBLANES, LANES), jnp.float32)
    keys = [(half, group) for half in range(halves) for group in range(groups)]

    def advance(chunk, carry):
        carry = list(carry)
        x_tiles = [tile_of(mixed, chunk, group) for group in range(groups)]
        z_tiles = [tile_of(slope, chunk, group) for group in range(groups)]
        back_tiles = [tile_of(slope, block // SUBLANES - 1 - chunk, group) for group in range(groups)]
        for inner in range(SUBLANES):
            x_rows = [spread(tile, inner) for tile in x_tiles]
            z_rows = [spread(tile, inner) for tile in z_tiles]
            back_rows = [spread(tile, SUBLANES - 1 - inner) for tile in back_tiles]
            for at, (half, group) in enumerate(keys):
                state, timed, plain_sum, timed_sum, back, back_timed = carry[at]
                step = steps[half, group]
                moved = step * state
                timed = step * timed + moved
                state = moved + x_rows[group]
                plain_sum = plain_sum + z_rows[group] * state
                timed_sum = timed_sum + z_rows[group] * timed
                back_moved = step * back
                back_timed = step * back_timed + back_moved
                back = back_moved + back_rows[group]
                carry[at] = (state, timed, plain_sum, timed_sum, back, back_timed)
        return tuple(carry)

    done = lax.fori_loop(0, block // SUBLANES, advance, tuple((zero,) * 6 for _ in keys))
    for at, (half, group) in enumerate(keys):
        state, timed, plain_sum, timed_sum, back, back_timed = done[at]
        step = steps[half, group]
        base = (group * modes + half * SUBLANES) * ROWS_OUT
        lanes = slice(group * LANES, (group + 1) * LANES)
        skip_part = jnp.sum(mixed[:, lanes] * slope[:, lanes], axis=0, keepdims=True)
        rows = (
            step * state,
            step * (timed + state),
            back,
            back_timed,
            plain_sum,
            timed_sum,
            jnp.broadcast_to(skip_part, (SUBLANES, LANES)),
            zero,
        )
        for row, value in enumerate(rows):
            out_ref[pl.ds(base + row, SUBLANES, stride=ROWS_OUT), :] = value


def local_kernel(key_ref, value_ref, gate_ref, grad_ref, res_ref, rate_ref, skip_ref, fwd_ref, bwd_ref, before, after, taps):
    block, width = key_ref.shape
    modes = rate_ref.shape[0]
    groups = width // LANES
    chunks = block // SUBLANES
    zero = jnp.zeros((SUBLANES, LANES), jnp.float32)
    within = lax.broadcasted_iota(jnp.int32, (SUBLANES, LANES), 0).astype(jnp.float32)
    for group in range(groups):
        lanes = slice(group * LANES, (group + 1) * LANES)
        before[group, 0:SUBLANES, :] = zero
        before[group, SUBLANES:, :] = key_ref[:, lanes].astype(jnp.float32) * value_ref[:, lanes].astype(jnp.float32)
        after[group, 0:block, :] = grad_ref[:, lanes].astype(jnp.float32) * gate_ref[:, lanes].astype(jnp.float32)
        after[group, block:, :] = zero
        rate = jnp.exp(rate_ref[:, lanes])
        amplitude = res_ref[:, lanes] * jnp.sqrt(2.0 * rate / modes)
        stride = jnp.exp(-SUBLANES * rate)
        totals = [zero] * chunks
        for mode in range(modes):
            one = slice(mode, mode + 1)
            wave = jnp.broadcast_to(amplitude[one], (SUBLANES, LANES)) * jnp.exp(
                -jnp.broadcast_to(rate[one], (SUBLANES, LANES)) * within
            )
            jump = jnp.broadcast_to(stride[one], (SUBLANES, LANES))
            for chunk in range(chunks):
                totals[chunk] = totals[chunk] + wave
                if chunk + 1 < chunks:
                    wave = wave * jump
        for chunk in range(chunks):
            taps[group, chunk * SUBLANES : (chunk + 1) * SUBLANES, :] = totals[chunk]

    for group in range(groups):
        lanes = slice(group * LANES, (group + 1) * LANES)
        skip_row = jnp.broadcast_to(skip_ref[:, lanes], (SUBLANES, LANES))
        ahead = [skip_row * before[group, (c + 1) * SUBLANES : (c + 2) * SUBLANES, :] for c in range(chunks)]
        for shift in range(SUBLANES):
            moved = [before[group, pl.ds((c + 1) * SUBLANES - shift, SUBLANES), :] for c in range(chunks)]
            for lag in range(chunks):
                tap = jnp.broadcast_to(taps[group, pl.ds(lag * SUBLANES + shift, 1), :], (SUBLANES, LANES))
                for chunk in range(lag, chunks):
                    ahead[chunk] = ahead[chunk] + tap * moved[chunk - lag]
        for chunk in range(chunks):
            fwd_ref[chunk * SUBLANES : (chunk + 1) * SUBLANES, lanes] = ahead[chunk]
        back = [skip_row * after[group, c * SUBLANES : (c + 1) * SUBLANES, :] for c in range(chunks)]
        for shift in range(SUBLANES):
            moved = [after[group, pl.ds(c * SUBLANES + shift, SUBLANES), :] for c in range(chunks)]
            for lag in range(chunks):
                tap = jnp.broadcast_to(taps[group, pl.ds(lag * SUBLANES + shift, 1), :], (SUBLANES, LANES))
                for chunk in range(chunks - lag):
                    back[chunk] = back[chunk] + tap * moved[chunk + lag]
        for chunk in range(chunks):
            bwd_ref[chunk * SUBLANES : (chunk + 1) * SUBLANES, lanes] = back[chunk]


def shifted(value, amount):
    rows = lax.broadcasted_iota(jnp.int32, value.shape, 0)
    moved = pltpu.roll(value, amount % value.shape[0], 0)
    keep = rows >= amount if amount > 0 else rows < value.shape[0] + amount
    return jnp.where(keep, moved, 0.0)


def scan_kernel(block, modes, in_ref, res_ref, rate_ref, out_ref):
    chunk = SUBLANES
    rate = jnp.broadcast_to(jnp.exp(rate_ref[...]), (SUBLANES, LANES))
    unit = jnp.sqrt(2.0 * rate / modes)
    amplitude = jnp.broadcast_to(res_ref[...], (SUBLANES, LANES)) * unit
    power = [jnp.exp(-float(block * v) * rate) for v in range(chunk)]
    decay = power[1]

    def load(v, row):
        return in_ref[pl.ds(v * ROWS_OUT + row, SUBLANES, stride=chunk * ROWS_OUT), :]

    zero = jnp.zeros((SUBLANES, LANES), jnp.float32)
    state, timed, back = zero, zero, zero
    states, timeds, backs = [], [], [None] * chunk
    for v in range(chunk):
        states.append(state)
        timeds.append(timed)
        moved = decay * state
        timed = decay * timed + float(block) * moved + load(v, 1)
        state = moved + load(v, 0)
    for v in reversed(range(chunk)):
        backs[v] = back
        back = decay * back + load(v, 2)
    span = block * chunk
    distance = 1
    while distance < SUBLANES:
        far = jnp.exp(-float(span * distance) * rate)
        older = far * shifted(state, distance)
        timed = timed + far * shifted(timed, distance) + float(span * distance) * older
        state = state + older
        back = back + far * shifted(back, -distance)
        distance *= 2
    state, timed, back = shifted(state, 1), shifted(timed, 1), shifted(back, -1)
    plain, slow, skip = zero, zero, zero
    for v in range(chunk):
        entering = states[v] + power[v] * state
        entering_timed = timeds[v] + power[v] * (timed + float(block * v) * state)
        leaving = backs[v] + power[chunk - 1 - v] * back
        slope, slope_timed = load(v, 2), load(v, 3)
        plain = plain + load(v, 4) + slope * entering
        slow = slow + load(v, 5) + slope_timed * entering + slope * entering_timed
        skip = skip + load(v, 6)
        out_ref[pl.ds(v * ROWS_BACK, SUBLANES, stride=chunk * ROWS_BACK), :] = entering
        out_ref[pl.ds(v * ROWS_BACK + 1, SUBLANES, stride=chunk * ROWS_BACK), :] = leaving

    def total(value):
        return jnp.broadcast_to(jnp.sum(value, axis=0, keepdims=True), (SUBLANES, LANES))

    plain, slow, skip = total(plain), total(slow), total(skip)
    raw_res = plain * unit
    raw_log = (0.5 * plain - rate * slow) * amplitude
    for v in range(chunk):
        for row, value in ((2, raw_res), (3, raw_log), (4, skip)):
            out_ref[pl.ds(v * ROWS_BACK + row, SUBLANES, stride=chunk * ROWS_BACK), :] = value


def square_kernel(modes, in_ref, res_ref, log_ref, skip_ref, out_ref):
    groups = res_ref.shape[1] // LANES
    total = jnp.zeros((SUBLANES, LANES), jnp.float32)
    for group in range(groups):
        lanes = slice(group * LANES, (group + 1) * LANES)
        for half in range(modes // SUBLANES):
            base = (group * modes + half * SUBLANES) * ROWS_BACK
            rows = slice(half * SUBLANES, (half + 1) * SUBLANES)
            for row, ref in ((2, res_ref), (3, log_ref)):
                value = in_ref[pl.ds(base + row, SUBLANES, stride=ROWS_BACK), :]
                ref[rows, lanes] = value
                total = total + value * value
        skip = in_ref[pl.ds(group * modes * ROWS_BACK + 4, 1), :]
        skip_ref[:, lanes] = skip
        first = lax.broadcasted_iota(jnp.int32, (SUBLANES, LANES), 0) == 0
        total = total + jnp.where(first, skip * skip, 0.0)
    out_ref[...] = jnp.broadcast_to(jnp.sum(total, axis=0, keepdims=True)[None], out_ref.shape)


def clip_kernel(count, squares_ref, res_ref, log_ref, skip_ref, out_res, out_log, out_skip):
    squares = jnp.sum(jnp.sum(squares_ref[...], axis=0), axis=1, keepdims=True)
    factor = CLIP_RMS / jnp.maximum(jnp.sqrt(squares / count), CLIP_RMS)
    out_res[...] = res_ref[...] * factor
    out_log[...] = log_ref[...] * factor
    out_skip[...] = skip_ref[...] * factor


def output_kernel(in_ref, fwd_ref, bwd_ref, key_ref, value_ref, gate_ref, grad_ref, res_ref, rate_ref, out_ref, gate_out, key_out, value_out):
    block, width = key_ref.shape
    modes = rate_ref.shape[0]
    groups = width // LANES
    chunks = block // SUBLANES
    within = lax.broadcasted_iota(jnp.int32, (SUBLANES, LANES), 0).astype(jnp.float32)
    for group in range(groups):
        lanes = slice(group * LANES, (group + 1) * LANES)
        rate = jnp.exp(rate_ref[:, lanes])
        amplitude = res_ref[:, lanes] * jnp.sqrt(2.0 * rate / modes)
        stride = jnp.exp(-SUBLANES * rate)
        ahead = [fwd_ref[c * SUBLANES : (c + 1) * SUBLANES, lanes] for c in range(chunks)]
        back = [bwd_ref[c * SUBLANES : (c + 1) * SUBLANES, lanes] for c in range(chunks)]
        for mode in range(modes):
            one = slice(mode, mode + 1)
            base = (group * modes + mode) * ROWS_BACK
            rate_row = jnp.broadcast_to(rate[one], (SUBLANES, LANES))
            jump = jnp.broadcast_to(stride[one], (SUBLANES, LANES))
            wave = jnp.broadcast_to(amplitude[one] * in_ref[pl.ds(base, 1), :], (SUBLANES, LANES)) * jnp.exp(-rate_row * within)
            echo = jnp.broadcast_to(amplitude[one] * in_ref[pl.ds(base + 1, 1), :], (SUBLANES, LANES)) * jnp.exp(
                -rate_row * (float(SUBLANES) - within)
            )
            for chunk in range(chunks):
                ahead[chunk] = ahead[chunk] + wave
                back[chunks - 1 - chunk] = back[chunks - 1 - chunk] + echo
                if chunk + 1 < chunks:
                    wave = wave * jump
                    echo = echo * jump
        for pair in range(chunks // 2):
            rows = slice(pair * 2 * SUBLANES, (pair + 1) * 2 * SUBLANES)
            filtered = jnp.concatenate([ahead[2 * pair], ahead[2 * pair + 1]], axis=0)
            mixed_grad = jnp.concatenate([back[2 * pair], back[2 * pair + 1]], axis=0)
            out_ref[rows, lanes] = (gate_ref[rows, lanes].astype(jnp.float32) * filtered).astype(jnp.bfloat16)
            gate_out[rows, lanes] = (grad_ref[rows, lanes].astype(jnp.float32) * filtered).astype(jnp.bfloat16)
            key_out[rows, lanes] = (value_ref[rows, lanes].astype(jnp.float32) * mixed_grad).astype(jnp.bfloat16)
            value_out[rows, lanes] = (key_ref[rows, lanes].astype(jnp.float32) * mixed_grad).astype(jnp.bfloat16)


def call(kernel, out_shape, *args, scratch=()):
    multiple = isinstance(out_shape, (tuple, list))
    return pl.pallas_call(
        kernel,
        out_shape=out_shape,
        in_specs=[VMEM] * len(args),
        out_specs=[VMEM] * len(out_shape) if multiple else VMEM,
        scratch_shapes=list(scratch),
        compiler_params=PARAMS,
    )(*args)


def floats(*shape):
    return jax.ShapeDtypeStruct(shape, jnp.float32)


def per_device(gate_in, key_in, value_in, out_grad, residue, log_rate, skip):
    block, width = gate_in.shape
    modes = residue.shape[0]
    blocks = lax.axis_size("seq")
    shards = lax.axis_size("chan")
    groups = width // LANES
    owners = groups * modes
    assert owners == blocks
    device = lax.axis_index("seq")
    own_mode, own_group = device % modes, device // modes
    own_rate = lax.dynamic_slice(log_rate, (own_mode, own_group * LANES), (1, LANES))
    own_res = lax.dynamic_slice(residue, (own_mode, own_group * LANES), (1, LANES))
    skip_row = skip.reshape(1, width)

    sent = call(
        summary_kernel,
        floats(owners * ROWS_OUT, LANES),
        key_in, value_in, gate_in, out_grad, log_rate,
        scratch=[pltpu.VMEM((block, width), jnp.float32)] * 2,
    )
    arrived = lax.all_to_all(sent.reshape(owners, ROWS_OUT, LANES), "seq", 0, 0, tiled=True)
    forward, backward = call(
        local_kernel,
        (floats(block, width), floats(block, width)),
        key_in, value_in, gate_in, out_grad, residue, log_rate, skip_row,
        scratch=[
            pltpu.VMEM((groups, block + SUBLANES, LANES), jnp.float32),
            pltpu.VMEM((groups, block + SUBLANES, LANES), jnp.float32),
            pltpu.VMEM((groups, block, LANES), jnp.float32),
        ],
    )
    reply = call(
        functools.partial(scan_kernel, block, modes),
        floats(blocks * ROWS_BACK, LANES),
        arrived.reshape(blocks * ROWS_OUT, LANES), own_res, own_rate,
    )
    states = lax.all_to_all(reply.reshape(blocks, ROWS_BACK, LANES), "seq", 0, 0, tiled=True)
    states = states.reshape(owners * ROWS_BACK, LANES)
    raw_res, raw_log, raw_skip, squares = call(
        functools.partial(square_kernel, modes),
        (floats(modes, width), floats(modes, width), floats(1, width), floats(shards, 1, LANES)),
        states,
    )
    squares = lax.all_to_all(squares, "chan", 0, 0, tiled=True)
    gated_out, gate_grad, key_grad, value_grad = call(
        output_kernel,
        (jax.ShapeDtypeStruct((block, width), jnp.bfloat16),) * 4,
        states, forward, backward, key_in, value_in, gate_in, out_grad, residue, log_rate,
    )
    residue_grad, log_rate_grad, skip_grad = call(
        functools.partial(clip_kernel, float((2 * modes + 1) * width * shards)),
        (floats(modes, width), floats(modes, width), floats(1, width)),
        squares, raw_res, raw_log, raw_skip,
    )
    return gated_out, gate_grad, key_grad, value_grad, residue_grad, log_rate_grad, skip_grad.reshape(width)


def solution(mesh):
    field, parameter, gain = P("seq", "chan"), P(None, "chan"), P("chan")
    return jax.shard_map(
        per_device,
        mesh=mesh,
        in_specs=(field, field, field, field, parameter, parameter, gain),
        out_specs=(field, field, field, field, parameter, parameter, gain),
        check_vma=False,
    )
```

```python
import functools

import jax
import jax.numpy as jnp
from jax import lax
from jax.experimental import pallas as pl
from jax.experimental.pallas import tpu as pltpu
from jax.sharding import PartitionSpec as P

CLIP_RMS = 1.0
LANES = 128
SUBLANES = 8
ROWS_OUT = 7
ROWS_BACK = 5
Y_RUN = 4
VMEM = pl.BlockSpec(memory_space=pltpu.VMEM)
PARAMS = pltpu.CompilerParams(vmem_limit_bytes=32 * 1024 * 1024)


def tile_of(ref, chunk, group):
    return ref[pl.ds(pl.multiple_of(chunk * SUBLANES, SUBLANES), SUBLANES), group * LANES : (group + 1) * LANES]


def spread(tile, row):
    return jnp.broadcast_to(tile[row : row + 1], (SUBLANES, LANES))


def summary_kernel(key_hbm, value_hbm, gate_hbm, grad_hbm, rate_hbm, out_ref, key_ref, value_ref, gate_ref, grad_ref, rate_ref, mixed, slope, sems):
    block, width = key_ref.shape
    modes = rate_ref.shape[0]
    halves, groups = modes // SUBLANES, width // LANES
    pairs = ((rate_hbm, rate_ref), (key_hbm, key_ref), (value_hbm, value_ref), (grad_hbm, grad_ref), (gate_hbm, gate_ref))
    copies = [pltpu.make_async_copy(source, target, sems.at[at]) for at, (source, target) in enumerate(pairs)]
    for copy in copies:
        copy.start()
    copies[0].wait()
    steps = {}
    for half in range(halves):
        for group in range(groups):
            rate = jnp.exp(rate_ref[half * SUBLANES : (half + 1) * SUBLANES, group * LANES : (group + 1) * LANES])
            steps[half, group] = jnp.exp(-rate)
    copies[1].wait()
    copies[2].wait()
    mixed[...] = key_ref[...].astype(jnp.float32) * value_ref[...].astype(jnp.float32)
    copies[3].wait()
    copies[4].wait()
    slope[...] = grad_ref[...].astype(jnp.float32) * gate_ref[...].astype(jnp.float32)
    zero = jnp.zeros((SUBLANES, LANES), jnp.float32)
    keys = [(half, group) for half in range(halves) for group in range(groups)]

    def advance(chunk, carry):
        carry = list(carry)
        x_tiles = [tile_of(mixed, chunk, group) for group in range(groups)]
        z_tiles = [tile_of(slope, chunk, group) for group in range(groups)]
        back_tiles = [tile_of(slope, block // SUBLANES - 1 - chunk, group) for group in range(groups)]
        for inner in range(SUBLANES):
            x_rows = [spread(tile, inner) for tile in x_tiles]
            z_rows = [spread(tile, inner) for tile in z_tiles]
            back_rows = [spread(tile, SUBLANES - 1 - inner) for tile in back_tiles]
            for at, (half, group) in enumerate(keys):
                state, timed, plain_sum, timed_sum, back, back_timed = carry[at]
                step = steps[half, group]
                moved = step * state
                timed = step * timed + moved
                state = moved + x_rows[group]
                plain_sum = plain_sum + z_rows[group] * state
                timed_sum = timed_sum + z_rows[group] * timed
                back_moved = step * back
                back_timed = step * back_timed + back_moved
                back = back_moved + back_rows[group]
                carry[at] = (state, timed, plain_sum, timed_sum, back, back_timed)
        return tuple(carry)

    done = lax.fori_loop(0, block // SUBLANES, advance, tuple((zero,) * 6 for _ in keys))
    for at, (half, group) in enumerate(keys):
        state, timed, plain_sum, timed_sum, back, back_timed = done[at]
        step = steps[half, group]
        base = (group * modes + half * SUBLANES) * ROWS_OUT
        lanes = slice(group * LANES, (group + 1) * LANES)
        skip_part = jnp.sum(mixed[:, lanes] * slope[:, lanes], axis=0, keepdims=True)
        rows = (
            step * state,
            step * (timed + state),
            back,
            back_timed,
            plain_sum,
            timed_sum,
            jnp.broadcast_to(skip_part, (SUBLANES, LANES)),
        )
        for row, value in enumerate(rows):
            out_ref[pl.ds(base + row, SUBLANES, stride=ROWS_OUT), :] = value


def local_kernel(key_ref, value_ref, gate_ref, grad_ref, res_ref, rate_ref, skip_ref, fwd_ref, bwd_ref, before, after, taps):
    block, width = key_ref.shape
    modes = rate_ref.shape[0]
    groups = width // LANES
    chunks = block // SUBLANES
    zero = jnp.zeros((SUBLANES, LANES), jnp.float32)
    within = lax.broadcasted_iota(jnp.int32, (SUBLANES, LANES), 0).astype(jnp.float32)
    for group in range(groups):
        lanes = slice(group * LANES, (group + 1) * LANES)
        before[group, 0:SUBLANES, :] = zero
        before[group, SUBLANES:, :] = key_ref[:, lanes].astype(jnp.float32) * value_ref[:, lanes].astype(jnp.float32)
        after[group, 0:block, :] = grad_ref[:, lanes].astype(jnp.float32) * gate_ref[:, lanes].astype(jnp.float32)
        after[group, block:, :] = zero
        rate = jnp.exp(rate_ref[:, lanes])
        amplitude = res_ref[:, lanes] * jnp.sqrt(2.0 * rate / modes)
        stride = jnp.exp(-SUBLANES * rate)
        totals = [zero] * chunks
        for mode in range(modes):
            one = slice(mode, mode + 1)
            wave = jnp.broadcast_to(amplitude[one], (SUBLANES, LANES)) * jnp.exp(
                -jnp.broadcast_to(rate[one], (SUBLANES, LANES)) * within
            )
            jump = jnp.broadcast_to(stride[one], (SUBLANES, LANES))
            for chunk in range(chunks):
                totals[chunk] = totals[chunk] + wave
                if chunk + 1 < chunks:
                    wave = wave * jump
        for chunk in range(chunks):
            taps[group, chunk * SUBLANES : (chunk + 1) * SUBLANES, :] = totals[chunk]

    for group in range(groups):
        lanes = slice(group * LANES, (group + 1) * LANES)
        skip_row = jnp.broadcast_to(skip_ref[:, lanes], (SUBLANES, LANES))
        ahead = [skip_row * before[group, (c + 1) * SUBLANES : (c + 2) * SUBLANES, :] for c in range(chunks)]
        for shift in range(SUBLANES):
            moved = [before[group, pl.ds((c + 1) * SUBLANES - shift, SUBLANES), :] for c in range(chunks)]
            for lag in range(chunks):
                tap = jnp.broadcast_to(taps[group, pl.ds(lag * SUBLANES + shift, 1), :], (SUBLANES, LANES))
                for chunk in range(lag, chunks):
                    ahead[chunk] = ahead[chunk] + tap * moved[chunk - lag]
        for chunk in range(chunks):
            fwd_ref[chunk * SUBLANES : (chunk + 1) * SUBLANES, lanes] = ahead[chunk]
        back = [skip_row * after[group, c * SUBLANES : (c + 1) * SUBLANES, :] for c in range(chunks)]
        for shift in range(SUBLANES):
            moved = [after[group, pl.ds(c * SUBLANES + shift, SUBLANES), :] for c in range(chunks)]
            for lag in range(chunks):
                tap = jnp.broadcast_to(taps[group, pl.ds(lag * SUBLANES + shift, 1), :], (SUBLANES, LANES))
                for chunk in range(chunks - lag):
                    back[chunk] = back[chunk] + tap * moved[chunk + lag]
        for chunk in range(chunks):
            bwd_ref[chunk * SUBLANES : (chunk + 1) * SUBLANES, lanes] = back[chunk]


def shifted(value, amount):
    rows = lax.broadcasted_iota(jnp.int32, value.shape, 0)
    moved = pltpu.roll(value, amount % value.shape[0], 0)
    keep = rows >= amount if amount > 0 else rows < value.shape[0] + amount
    return jnp.where(keep, moved, 0.0)


def scan_kernel(block, modes, in_ref, res_ref, rate_ref, out_ref):
    chunk = SUBLANES
    rate = jnp.broadcast_to(jnp.exp(rate_ref[...]), (SUBLANES, LANES))
    unit = jnp.sqrt(2.0 * rate / modes)
    amplitude = jnp.broadcast_to(res_ref[...], (SUBLANES, LANES)) * unit
    power = [jnp.exp(-float(block * v) * rate) for v in range(chunk)]
    decay = power[1]

    def load(v, row):
        return in_ref[pl.ds(v * ROWS_OUT + row, SUBLANES, stride=chunk * ROWS_OUT), :]

    zero = jnp.zeros((SUBLANES, LANES), jnp.float32)
    state, timed, back = zero, zero, zero
    states, timeds, backs = [], [], [None] * chunk
    for v in range(chunk):
        states.append(state)
        timeds.append(timed)
        moved = decay * state
        timed = decay * timed + float(block) * moved + load(v, 1)
        state = moved + load(v, 0)
    for v in reversed(range(chunk)):
        backs[v] = back
        back = decay * back + load(v, 2)
    span = block * chunk
    distance = 1
    while distance < SUBLANES:
        far = jnp.exp(-float(span * distance) * rate)
        older = far * shifted(state, distance)
        timed = timed + far * shifted(timed, distance) + float(span * distance) * older
        state = state + older
        back = back + far * shifted(back, -distance)
        distance *= 2
    state, timed, back = shifted(state, 1), shifted(timed, 1), shifted(back, -1)
    plain, slow, skip = zero, zero, zero
    for v in range(chunk):
        entering = states[v] + power[v] * state
        entering_timed = timeds[v] + power[v] * (timed + float(block * v) * state)
        leaving = backs[v] + power[chunk - 1 - v] * back
        slope, slope_timed = load(v, 2), load(v, 3)
        plain = plain + load(v, 4) + slope * entering
        slow = slow + load(v, 5) + slope_timed * entering + slope * entering_timed
        skip = skip + load(v, 6)
        out_ref[pl.ds(v * ROWS_BACK, SUBLANES, stride=chunk * ROWS_BACK), :] = entering
        out_ref[pl.ds(v * ROWS_BACK + 1, SUBLANES, stride=chunk * ROWS_BACK), :] = leaving

    def total(value):
        return jnp.broadcast_to(jnp.sum(value, axis=0, keepdims=True), (SUBLANES, LANES))

    plain, slow, skip = total(plain), total(slow), total(skip)
    raw_res = plain * unit
    raw_log = (0.5 * plain - rate * slow) * amplitude
    for v in range(chunk):
        for row, value in ((2, raw_res), (3, raw_log), (4, skip)):
            out_ref[pl.ds(v * ROWS_BACK + row, SUBLANES, stride=chunk * ROWS_BACK), :] = value


def square_kernel(modes, in_ref, res_ref, log_ref, skip_ref, out_ref):
    groups = res_ref.shape[1] // LANES
    total = jnp.zeros((SUBLANES, LANES), jnp.float32)
    for group in range(groups):
        lanes = slice(group * LANES, (group + 1) * LANES)
        for half in range(modes // SUBLANES):
            base = (group * modes + half * SUBLANES) * ROWS_BACK
            rows = slice(half * SUBLANES, (half + 1) * SUBLANES)
            for row, ref in ((2, res_ref), (3, log_ref)):
                value = in_ref[pl.ds(base + row, SUBLANES, stride=ROWS_BACK), :]
                ref[rows, lanes] = value
                total = total + value * value
        skip = in_ref[pl.ds(group * modes * ROWS_BACK + 4, 1), :]
        skip_ref[:, lanes] = skip
        first = lax.broadcasted_iota(jnp.int32, (SUBLANES, LANES), 0) == 0
        total = total + jnp.where(first, skip * skip, 0.0)
    out_ref[...] = jnp.broadcast_to(jnp.sum(total, axis=0, keepdims=True), out_ref.shape)


def clip_kernel(count, squares_ref, res_ref, log_ref, skip_ref, out_res, out_log, out_skip):
    squares = jnp.sum(jnp.sum(squares_ref[...], axis=0, keepdims=True), axis=1, keepdims=True)
    factor = CLIP_RMS / jnp.maximum(jnp.sqrt(squares / count), CLIP_RMS)
    out_res[...] = res_ref[...] * factor
    out_log[...] = log_ref[...] * factor
    out_skip[...] = skip_ref[...] * factor


def output_kernel(in_ref, fwd_ref, bwd_ref, key_ref, value_ref, gate_ref, grad_ref, res_ref, rate_ref, out_ref, gate_out, key_out, value_out):
    block, width = key_ref.shape
    modes = rate_ref.shape[0]
    groups = width // LANES
    chunks = block // SUBLANES
    within = lax.broadcasted_iota(jnp.int32, (SUBLANES, LANES), 0).astype(jnp.float32)
    for group in range(groups):
        lanes = slice(group * LANES, (group + 1) * LANES)
        rate = jnp.exp(rate_ref[:, lanes])
        amplitude = res_ref[:, lanes] * jnp.sqrt(2.0 * rate / modes)
        stride = jnp.exp(-SUBLANES * rate)
        ahead = [fwd_ref[c * SUBLANES : (c + 1) * SUBLANES, lanes] for c in range(chunks)]
        back = [bwd_ref[c * SUBLANES : (c + 1) * SUBLANES, lanes] for c in range(chunks)]
        for mode in range(modes):
            one = slice(mode, mode + 1)
            base = (group * modes + mode) * ROWS_BACK
            rate_row = jnp.broadcast_to(rate[one], (SUBLANES, LANES))
            jump = jnp.broadcast_to(stride[one], (SUBLANES, LANES))
            wave = jnp.broadcast_to(amplitude[one] * in_ref[pl.ds(base, 1), :], (SUBLANES, LANES)) * jnp.exp(-rate_row * within)
            echo = jnp.broadcast_to(amplitude[one] * in_ref[pl.ds(base + 1, 1), :], (SUBLANES, LANES)) * jnp.exp(
                -rate_row * (float(SUBLANES) - within)
            )
            for chunk in range(chunks):
                ahead[chunk] = ahead[chunk] + wave
                back[chunks - 1 - chunk] = back[chunks - 1 - chunk] + echo
                if chunk + 1 < chunks:
                    wave = wave * jump
                    echo = echo * jump
        for pair in range(chunks // 2):
            rows = slice(pair * 2 * SUBLANES, (pair + 1) * 2 * SUBLANES)
            filtered = jnp.concatenate([ahead[2 * pair], ahead[2 * pair + 1]], axis=0)
            mixed_grad = jnp.concatenate([back[2 * pair], back[2 * pair + 1]], axis=0)
            out_ref[rows, lanes] = (gate_ref[rows, lanes].astype(jnp.float32) * filtered).astype(jnp.bfloat16)
            gate_out[rows, lanes] = (grad_ref[rows, lanes].astype(jnp.float32) * filtered).astype(jnp.bfloat16)
            key_out[rows, lanes] = (value_ref[rows, lanes].astype(jnp.float32) * mixed_grad).astype(jnp.bfloat16)
            value_out[rows, lanes] = (key_ref[rows, lanes].astype(jnp.float32) * mixed_grad).astype(jnp.bfloat16)


def in_hbm(*arrays):
    return tuple(pltpu.with_memory_space_constraint(array, pltpu.HBM) for array in arrays)


def call(kernel, out_shape, *args, scratch=(), space=VMEM):
    multiple = isinstance(out_shape, (tuple, list))
    return pl.pallas_call(
        kernel,
        out_shape=out_shape,
        in_specs=[space] * len(args),
        out_specs=[VMEM] * len(out_shape) if multiple else VMEM,
        scratch_shapes=list(scratch),
        compiler_params=PARAMS,
    )(*args)


def exchange(rows, axis, groups=None):
    count, lanes = rows.shape
    moved = lax.all_to_all(rows.reshape(count, 1, lanes), axis, 0, 0, axis_index_groups=groups, tiled=True)
    return moved.reshape(count, lanes)


def near_groups(blocks, shards):
    run = blocks // Y_RUN
    groups = []
    for device in range(blocks):
        other = device ^ (2 * run)
        groups.append([(other if shard % 2 else device) * shards + shard for shard in range(shards)])
    return groups


def floats(*shape):
    return jax.ShapeDtypeStruct(shape, jnp.float32)


def per_device(gate_in, key_in, value_in, out_grad, residue, log_rate, skip):
    block, width = gate_in.shape
    modes = residue.shape[0]
    blocks = lax.axis_size("seq")
    shards = lax.axis_size("chan")
    groups = width // LANES
    owners = groups * modes
    assert owners == blocks
    device = lax.axis_index("seq")
    own_mode, own_group = device % modes, device // modes
    own_rate = lax.dynamic_slice(log_rate, (own_mode, own_group * LANES), (1, LANES))
    own_res = lax.dynamic_slice(residue, (own_mode, own_group * LANES), (1, LANES))
    skip_row = skip.reshape(1, width)

    sent = call(
        summary_kernel,
        floats(owners * ROWS_OUT, LANES),
        *in_hbm(key_in, value_in, gate_in, out_grad, log_rate),
        scratch=[pltpu.VMEM((block, width), jnp.bfloat16)] * 4
        + [pltpu.VMEM((modes, width), jnp.float32)]
        + [pltpu.VMEM((block, width), jnp.float32)] * 2
        + [pltpu.SemaphoreType.DMA((5,))],
        space=pl.BlockSpec(memory_space=pltpu.HBM),
    )
    arrived = exchange(sent, "seq")
    forward, backward = call(
        local_kernel,
        (floats(block, width), floats(block, width)),
        key_in, value_in, gate_in, out_grad, residue, log_rate, skip_row,
        scratch=[
            pltpu.VMEM((groups, block + SUBLANES, LANES), jnp.float32),
            pltpu.VMEM((groups, block + SUBLANES, LANES), jnp.float32),
            pltpu.VMEM((groups, block, LANES), jnp.float32),
        ],
    )
    arrived, forward, backward = lax.optimization_barrier((arrived, forward, backward))
    reply = call(
        functools.partial(scan_kernel, block, modes),
        floats(blocks * ROWS_BACK, LANES),
        arrived, own_res, own_rate,
    )
    states = exchange(reply, "seq")
    raw_res, raw_log, raw_skip, squares = call(
        functools.partial(square_kernel, modes),
        (floats(modes, width), floats(modes, width), floats(1, width), floats(shards, LANES)),
        states,
    )
    squares = exchange(squares, ("seq", "chan"), near_groups(blocks, shards))
    gated_out, gate_grad, key_grad, value_grad = call(
        output_kernel,
        (jax.ShapeDtypeStruct((block, width), jnp.bfloat16),) * 4,
        states, forward, backward, key_in, value_in, gate_in, out_grad, residue, log_rate,
    )
    residue_grad, log_rate_grad, skip_grad = call(
        functools.partial(clip_kernel, float((2 * modes + 1) * width * shards)),
        (floats(modes, width), floats(modes, width), floats(1, width)),
        squares, raw_res, raw_log, raw_skip,
    )
    return gated_out, gate_grad, key_grad, value_grad, residue_grad, log_rate_grad, skip_grad.reshape(width)


def solution(mesh):
    field, parameter, gain = P("seq", "chan"), P(None, "chan"), P("chan")
    return jax.shard_map(
        per_device,
        mesh=mesh,
        in_specs=(field, field, field, field, parameter, parameter, gain),
        out_specs=(field, field, field, field, parameter, parameter, gain),
        check_vma=False,
    )
```

```python
import functools

import jax
import jax.numpy as jnp
from jax import lax
from jax.experimental import pallas as pl
from jax.experimental.pallas import tpu as pltpu
from jax.sharding import PartitionSpec as P

CLIP_RMS = 1.0
LANES = 128
SUBLANES = 8
ROWS_OUT = 7
ROWS_BACK = 5
Y_RUN = 4
LEADS = (46, 46)
ROOT_HIGH = 5
GROUPS_AT_ONCE = 2
VMEM = pl.BlockSpec(memory_space=pltpu.VMEM)
PARAMS = pltpu.CompilerParams(vmem_limit_bytes=32 * 1024 * 1024)


def tile_of(ref, chunk, group):
    return ref[pl.ds(pl.multiple_of(chunk * SUBLANES, SUBLANES), SUBLANES), group * LANES : (group + 1) * LANES]


def spread(tile, row):
    return jnp.broadcast_to(tile[row : row + 1], (SUBLANES, LANES))


def summary_kernel(key_hbm, value_hbm, gate_hbm, grad_hbm, rate_hbm, out_ref, key_ref, value_ref, gate_ref, grad_ref, rate_ref, mixed, slope, sems):
    block, width = key_ref.shape
    modes = rate_ref.shape[0]
    halves, groups = modes // SUBLANES, width // LANES
    pairs = ((rate_hbm, rate_ref), (key_hbm, key_ref), (value_hbm, value_ref), (grad_hbm, grad_ref), (gate_hbm, gate_ref))
    copies = [pltpu.make_async_copy(source, target, sems.at[at]) for at, (source, target) in enumerate(pairs)]
    for copy in copies:
        copy.start()
    copies[0].wait()
    steps = {}
    for half in range(halves):
        for group in range(groups):
            rate = jnp.exp(rate_ref[half * SUBLANES : (half + 1) * SUBLANES, group * LANES : (group + 1) * LANES])
            steps[half, group] = jnp.exp(-rate)
    copies[1].wait()
    copies[2].wait()
    mixed[...] = key_ref[...].astype(jnp.float32) * value_ref[...].astype(jnp.float32)
    copies[3].wait()
    copies[4].wait()
    slope[...] = grad_ref[...].astype(jnp.float32) * gate_ref[...].astype(jnp.float32)
    zero = jnp.zeros((SUBLANES, LANES), jnp.float32)
    for first in range(0, groups, GROUPS_AT_ONCE):
        held = range(first, first + GROUPS_AT_ONCE)
        keys = [(half, group) for half in range(halves) for group in held]

        def advance(chunk, carry):
            carry = list(carry)
            x_tiles = {group: tile_of(mixed, chunk, group) for group in held}
            z_tiles = {group: tile_of(slope, chunk, group) for group in held}
            back_tiles = {group: tile_of(slope, block // SUBLANES - 1 - chunk, group) for group in held}
            for inner in range(SUBLANES):
                x_rows = {group: spread(x_tiles[group], inner) for group in held}
                z_rows = {group: spread(z_tiles[group], inner) for group in held}
                back_rows = {group: spread(back_tiles[group], SUBLANES - 1 - inner) for group in held}
                for at, (half, group) in enumerate(keys):
                    state, timed, plain_sum, timed_sum, back, back_timed = carry[at]
                    step = steps[half, group]
                    moved = step * state
                    timed = step * timed + moved
                    state = moved + x_rows[group]
                    plain_sum = plain_sum + z_rows[group] * state
                    timed_sum = timed_sum + z_rows[group] * timed
                    back_moved = step * back
                    back_timed = step * back_timed + back_moved
                    back = back_moved + back_rows[group]
                    carry[at] = (state, timed, plain_sum, timed_sum, back, back_timed)
            return tuple(carry)

        done = lax.fori_loop(0, block // SUBLANES, advance, tuple((zero,) * 6 for _ in keys))
        for at, (half, group) in enumerate(keys):
            state, timed, plain_sum, timed_sum, back, back_timed = done[at]
            step = steps[half, group]
            base = (group * modes + half * SUBLANES) * ROWS_OUT
            lanes = slice(group * LANES, (group + 1) * LANES)
            skip_part = jnp.sum(mixed[:, lanes] * slope[:, lanes], axis=0, keepdims=True)
            rows = (
                step * state,
                step * (timed + state),
                back,
                back_timed,
                plain_sum,
                timed_sum,
                jnp.broadcast_to(skip_part, (SUBLANES, LANES)),
            )
            for row, value in enumerate(rows):
                out_ref[pl.ds(base + row, SUBLANES, stride=ROWS_OUT), :] = value


def local_kernel(key_ref, value_ref, gate_ref, grad_ref, res_ref, rate_ref, skip_ref, fwd_ref, bwd_ref, before, after, taps):
    block, width = key_ref.shape
    modes = rate_ref.shape[0]
    groups = width // LANES
    chunks = block // SUBLANES
    zero = jnp.zeros((SUBLANES, LANES), jnp.float32)
    within = lax.broadcasted_iota(jnp.int32, (SUBLANES, LANES), 0).astype(jnp.float32)
    for group in range(groups):
        lanes = slice(group * LANES, (group + 1) * LANES)
        before[group, 0:SUBLANES, :] = zero
        before[group, SUBLANES:, :] = key_ref[:, lanes].astype(jnp.float32) * value_ref[:, lanes].astype(jnp.float32)
        after[group, 0:block, :] = grad_ref[:, lanes].astype(jnp.float32) * gate_ref[:, lanes].astype(jnp.float32)
        after[group, block:, :] = zero
        rate = jnp.exp(rate_ref[:, lanes])
        amplitude = res_ref[:, lanes] * jnp.sqrt(2.0 * rate / modes)
        stride = jnp.exp(-SUBLANES * rate)
        totals = [zero] * chunks
        for mode in range(modes):
            one = slice(mode, mode + 1)
            wave = jnp.broadcast_to(amplitude[one], (SUBLANES, LANES)) * jnp.exp(
                -jnp.broadcast_to(rate[one], (SUBLANES, LANES)) * within
            )
            jump = jnp.broadcast_to(stride[one], (SUBLANES, LANES))
            for chunk in range(chunks):
                totals[chunk] = totals[chunk] + wave
                if chunk + 1 < chunks:
                    wave = wave * jump
        for chunk in range(chunks):
            taps[group, chunk * SUBLANES : (chunk + 1) * SUBLANES, :] = totals[chunk]

    for group in range(groups):
        lanes = slice(group * LANES, (group + 1) * LANES)
        skip_row = jnp.broadcast_to(skip_ref[:, lanes], (SUBLANES, LANES))
        ahead = [skip_row * before[group, (c + 1) * SUBLANES : (c + 2) * SUBLANES, :] for c in range(chunks)]
        for shift in range(SUBLANES):
            moved = [before[group, pl.ds((c + 1) * SUBLANES - shift, SUBLANES), :] for c in range(chunks)]
            for lag in range(chunks):
                tap = jnp.broadcast_to(taps[group, pl.ds(lag * SUBLANES + shift, 1), :], (SUBLANES, LANES))
                for chunk in range(lag, chunks):
                    ahead[chunk] = ahead[chunk] + tap * moved[chunk - lag]
        for chunk in range(chunks):
            fwd_ref[chunk * SUBLANES : (chunk + 1) * SUBLANES, lanes] = ahead[chunk]
        back = [skip_row * after[group, c * SUBLANES : (c + 1) * SUBLANES, :] for c in range(chunks)]
        for shift in range(SUBLANES):
            moved = [after[group, pl.ds(c * SUBLANES + shift, SUBLANES), :] for c in range(chunks)]
            for lag in range(chunks):
                tap = jnp.broadcast_to(taps[group, pl.ds(lag * SUBLANES + shift, 1), :], (SUBLANES, LANES))
                for chunk in range(chunks - lag):
                    back[chunk] = back[chunk] + tap * moved[chunk + lag]
        for chunk in range(chunks):
            bwd_ref[chunk * SUBLANES : (chunk + 1) * SUBLANES, lanes] = back[chunk]


def shifted(value, amount):
    rows = lax.broadcasted_iota(jnp.int32, value.shape, 0)
    moved = pltpu.roll(value, amount % value.shape[0], 0)
    keep = rows >= amount if amount > 0 else rows < value.shape[0] + amount
    return jnp.where(keep, moved, 0.0)


def scan_kernel(block, modes, lead, shift, in_ref, res_ref, rate_ref, out_ref):
    chunk = SUBLANES
    turn, cut = divmod(-lead % (chunk * SUBLANES), chunk)
    seam = lax.broadcasted_iota(jnp.int32, (SUBLANES, LANES), 0) == turn
    rate = jnp.broadcast_to(jnp.exp(rate_ref[...]), (SUBLANES, LANES))
    unit = jnp.sqrt(2.0 * rate / modes)
    amplitude = jnp.broadcast_to(res_ref[...], (SUBLANES, LANES)) * unit
    power = [jnp.exp(-float(block * v) * rate) for v in range(chunk)]
    decay = power[1]

    def load(v, row):
        return in_ref[pl.ds(v * ROWS_OUT + row, SUBLANES, stride=chunk * ROWS_OUT), :]

    zero = jnp.zeros((SUBLANES, LANES), jnp.float32)
    state, timed, back = zero, zero, zero
    states, timeds, backs = [], [], [None] * chunk
    for v in range(chunk):
        if v == cut:
            state, timed = jnp.where(seam, 0.0, state), jnp.where(seam, 0.0, timed)
        states.append(state)
        timeds.append(timed)
        moved = decay * state
        timed = decay * timed + float(block) * moved + load(v, 1)
        state = moved + load(v, 0)
    for v in reversed(range(chunk)):
        backs[v] = back
        back = decay * back + load(v, 2)
        if v == cut:
            back = jnp.where(seam, 0.0, back)
    state, timed = (pltpu.roll(value, -turn % SUBLANES, 0) for value in (state, timed))
    back = pltpu.roll(back, (SUBLANES - 1 - turn) % SUBLANES, 0)
    span = block * chunk
    distance = 1
    while distance < SUBLANES:
        far = jnp.exp(-float(span * distance) * rate)
        older = far * shifted(state, distance)
        timed = timed + far * shifted(timed, distance) + float(span * distance) * older
        state = state + older
        back = back + far * shifted(back, -distance)
        distance *= 2
    state, timed = (pltpu.roll(value, (turn + 1) % SUBLANES, 0) for value in (state, timed))
    back = pltpu.roll(back, turn, 0)
    start_state, start_timed = jnp.where(seam, 0.0, state), jnp.where(seam, 0.0, timed)
    end_back = jnp.where(seam, 0.0, back)
    plain, slow, skip = zero, zero, zero
    for v in range(chunk):
        before, before_timed = (start_state, start_timed) if v >= cut else (state, timed)
        entering = states[v] + power[v] * before
        entering_timed = timeds[v] + power[v] * (before_timed + float(block * v) * before)
        leaving = backs[v] + power[chunk - 1 - v] * (back if v >= cut else end_back)
        slope, slope_timed = load(v, 2), load(v, 3)
        plain = plain + load(v, 4) + slope * entering
        slow = slow + load(v, 5) + slope_timed * entering + slope * entering_timed
        skip = skip + load(v, 6)
        rows, place = divmod(v + shift, chunk)
        for row, value in ((0, entering), (1, leaving)):
            value = pltpu.roll(value, rows % SUBLANES, 0) if rows % SUBLANES else value
            out_ref[pl.ds(place * ROWS_BACK + row, SUBLANES, stride=chunk * ROWS_BACK), :] = value

    def total(value):
        return jnp.broadcast_to(jnp.sum(value, axis=0, keepdims=True), (SUBLANES, LANES))

    plain, slow, skip = total(plain), total(slow), total(skip)
    raw_res = plain * unit
    raw_log = (0.5 * plain - rate * slow) * amplitude
    for v in range(chunk):
        for row, value in ((2, raw_res), (3, raw_log), (4, skip)):
            out_ref[pl.ds(v * ROWS_BACK + row, SUBLANES, stride=chunk * ROWS_BACK), :] = value


def square_kernel(modes, shift, in_ref, res_ref, log_ref, skip_ref, out_ref):
    groups = res_ref.shape[1] // LANES
    runs = groups * modes // SUBLANES
    total = jnp.zeros((SUBLANES, LANES), jnp.float32)
    sublane = lax.broadcasted_iota(jnp.int32, (SUBLANES, LANES), 0)
    skipped, turn = divmod(shift, SUBLANES)
    for row, ref in ((2, res_ref), (3, log_ref)):
        tiles = [in_ref[pl.ds(run * SUBLANES * ROWS_BACK + row, SUBLANES, stride=ROWS_BACK), :] for run in range(runs)]
        if turn:
            turned = [pltpu.roll(tile, SUBLANES - turn, 0) for tile in tiles]
            tiles = [jnp.where(sublane < SUBLANES - turn, turned[run], turned[(run + 1) % runs]) for run in range(runs)]
        for run in range(runs):
            group, half = divmod(run, modes // SUBLANES)
            value = tiles[(run + skipped) % runs]
            ref[half * SUBLANES : (half + 1) * SUBLANES, group * LANES : (group + 1) * LANES] = value
            total = total + value * value
    for group in range(groups):
        at = (group * modes + shift) % (groups * modes)
        skip = in_ref[pl.ds(at * ROWS_BACK + 4, 1), :]
        skip_ref[:, group * LANES : (group + 1) * LANES] = skip
        total = total + jnp.where(sublane == 0, skip * skip, 0.0)
    out_ref[...] = jnp.broadcast_to(jnp.sum(total, axis=0, keepdims=True), out_ref.shape)


def clip_kernel(count, squares_ref, res_ref, log_ref, skip_ref, out_res, out_log, out_skip):
    squares = jnp.sum(jnp.sum(squares_ref[...], axis=0, keepdims=True), axis=1, keepdims=True)
    factor = CLIP_RMS / jnp.maximum(jnp.sqrt(squares / count), CLIP_RMS)
    out_res[...] = res_ref[...] * factor
    out_log[...] = log_ref[...] * factor
    out_skip[...] = skip_ref[...] * factor


def output_kernel(shift, in_ref, fwd_ref, bwd_ref, key_ref, value_ref, gate_ref, grad_ref, res_ref, rate_ref, out_ref, gate_out, key_out, value_out):
    block, width = key_ref.shape
    modes = rate_ref.shape[0]
    groups = width // LANES
    chunks = block // SUBLANES
    within = lax.broadcasted_iota(jnp.int32, (SUBLANES, LANES), 0).astype(jnp.float32)
    for group in range(groups):
        lanes = slice(group * LANES, (group + 1) * LANES)
        rate = jnp.exp(rate_ref[:, lanes])
        amplitude = res_ref[:, lanes] * jnp.sqrt(2.0 * rate / modes)
        stride = jnp.exp(-SUBLANES * rate)
        ahead = [fwd_ref[c * SUBLANES : (c + 1) * SUBLANES, lanes] for c in range(chunks)]
        back = [bwd_ref[c * SUBLANES : (c + 1) * SUBLANES, lanes] for c in range(chunks)]
        for mode in range(modes):
            one = slice(mode, mode + 1)
            base = (group * modes + mode + shift) % (groups * modes) * ROWS_BACK
            rate_row = jnp.broadcast_to(rate[one], (SUBLANES, LANES))
            jump = jnp.broadcast_to(stride[one], (SUBLANES, LANES))
            wave = jnp.broadcast_to(amplitude[one] * in_ref[pl.ds(base, 1), :], (SUBLANES, LANES)) * jnp.exp(-rate_row * within)
            echo = jnp.broadcast_to(amplitude[one] * in_ref[pl.ds(base + 1, 1), :], (SUBLANES, LANES)) * jnp.exp(
                -rate_row * (float(SUBLANES) - within)
            )
            for chunk in range(chunks):
                ahead[chunk] = ahead[chunk] + wave
                back[chunks - 1 - chunk] = back[chunks - 1 - chunk] + echo
                if chunk + 1 < chunks:
                    wave = wave * jump
                    echo = echo * jump
        for pair in range(chunks // 2):
            rows = slice(pair * 2 * SUBLANES, (pair + 1) * 2 * SUBLANES)
            filtered = jnp.concatenate([ahead[2 * pair], ahead[2 * pair + 1]], axis=0)
            mixed_grad = jnp.concatenate([back[2 * pair], back[2 * pair + 1]], axis=0)
            out_ref[rows, lanes] = (gate_ref[rows, lanes].astype(jnp.float32) * filtered).astype(jnp.bfloat16)
            gate_out[rows, lanes] = (grad_ref[rows, lanes].astype(jnp.float32) * filtered).astype(jnp.bfloat16)
            key_out[rows, lanes] = (value_ref[rows, lanes].astype(jnp.float32) * mixed_grad).astype(jnp.bfloat16)
            value_out[rows, lanes] = (key_ref[rows, lanes].astype(jnp.float32) * mixed_grad).astype(jnp.bfloat16)


def in_hbm(*arrays):
    return tuple(pltpu.with_memory_space_constraint(array, pltpu.HBM) for array in arrays)


def call(kernel, out_shape, *args, scratch=(), space=VMEM):
    multiple = isinstance(out_shape, (tuple, list))
    return pl.pallas_call(
        kernel,
        out_shape=out_shape,
        in_specs=[space] * len(args),
        out_specs=[VMEM] * len(out_shape) if multiple else VMEM,
        scratch_shapes=list(scratch),
        compiler_params=PARAMS,
    )(*args)


def exchange(rows, axis, groups=None):
    count, lanes = rows.shape
    moved = lax.all_to_all(rows.reshape(count, 1, lanes), axis, 0, 0, axis_index_groups=groups, tiled=True)
    return moved.reshape(count, lanes)


def near_groups(blocks, shards):
    run = blocks // Y_RUN
    groups = []
    for device in range(blocks):
        other = device ^ (2 * run)
        members = [(other if shard % 2 else device) * shards + shard for shard in range(shards)]
        groups.append(members[ROOT_HIGH:] + members[:ROOT_HIGH])
    return groups


def floats(*shape):
    return jax.ShapeDtypeStruct(shape, jnp.float32)


def summarize(key_in, value_in, gate_in, out_grad, log_rate):
    block, width = key_in.shape
    modes = log_rate.shape[0]
    return call(
        summary_kernel,
        floats(modes * (width // LANES) * ROWS_OUT, LANES),
        *in_hbm(key_in, value_in, gate_in, out_grad, log_rate),
        scratch=[pltpu.VMEM((block, width), jnp.bfloat16)] * 4
        + [pltpu.VMEM((modes, width), jnp.float32)]
        + [pltpu.VMEM((block, width), jnp.float32)] * 2
        + [pltpu.SemaphoreType.DMA((5,))],
        space=pl.BlockSpec(memory_space=pltpu.HBM),
    )


def per_device(gate_in, key_in, value_in, out_grad, residue, log_rate, skip):
    block, width = gate_in.shape
    modes = residue.shape[0]
    blocks = lax.axis_size("seq")
    shards = lax.axis_size("chan")
    groups = width // LANES
    owners = groups * modes
    assert owners == blocks
    device = lax.axis_index("seq")
    lead, reply_lead = LEADS
    shift = (lead - reply_lead) % blocks
    order = [(lead + at) % blocks for at in range(blocks)]
    reply_order = [(reply_lead + at) % blocks for at in range(blocks)]
    place = (device - lead) % blocks
    own_mode, own_group = place % modes, place // modes
    own_rate = lax.dynamic_slice(log_rate, (own_mode, own_group * LANES), (1, LANES))
    own_res = lax.dynamic_slice(residue, (own_mode, own_group * LANES), (1, LANES))
    skip_row = skip.reshape(1, width)

    sent = summarize(key_in, value_in, gate_in, out_grad, log_rate)
    arrived = exchange(sent, "seq", [order])
    forward, backward = call(
        local_kernel,
        (floats(block, width), floats(block, width)),
        key_in, value_in, gate_in, out_grad, residue, log_rate, skip_row,
        scratch=[
            pltpu.VMEM((groups, block + SUBLANES, LANES), jnp.float32),
            pltpu.VMEM((groups, block + SUBLANES, LANES), jnp.float32),
            pltpu.VMEM((groups, block, LANES), jnp.float32),
        ],
    )
    arrived, forward, backward = lax.optimization_barrier((arrived, forward, backward))
    reply = call(
        functools.partial(scan_kernel, block, modes, lead, shift),
        floats(blocks * ROWS_BACK, LANES),
        arrived, own_res, own_rate,
    )
    states = exchange(reply, "seq", [reply_order])
    raw_res, raw_log, raw_skip, squares = call(
        functools.partial(square_kernel, modes, shift),
        (floats(modes, width), floats(modes, width), floats(1, width), floats(shards, LANES)),
        states,
    )
    squares = exchange(squares, ("seq", "chan"), near_groups(blocks, shards))
    gated_out, gate_grad, key_grad, value_grad = call(
        functools.partial(output_kernel, shift),
        (jax.ShapeDtypeStruct((block, width), jnp.bfloat16),) * 4,
        states, forward, backward, key_in, value_in, gate_in, out_grad, residue, log_rate,
    )
    residue_grad, log_rate_grad, skip_grad = call(
        functools.partial(clip_kernel, float((2 * modes + 1) * width * shards)),
        (floats(modes, width), floats(modes, width), floats(1, width)),
        squares, raw_res, raw_log, raw_skip,
    )
    return gated_out, gate_grad, key_grad, value_grad, residue_grad, log_rate_grad, skip_grad.reshape(width)


def solution(mesh):
    field, parameter, gain = P("seq", "chan"), P(None, "chan"), P("chan")
    return jax.shard_map(
        per_device,
        mesh=mesh,
        in_specs=(field, field, field, field, parameter, parameter, gain),
        out_specs=(field, field, field, field, parameter, parameter, gain),
        check_vma=False,
    )
```

```python
import functools

import jax
import jax.numpy as jnp
from jax import lax
from jax.experimental import pallas as pl
from jax.experimental.pallas import tpu as pltpu
from jax.sharding import PartitionSpec as P

CLIP_RMS = 1.0
LANES = 128
SUBLANES = 8
ROWS_OUT = 7
ROWS_BACK = 5
Y_RUN = 4
LEAD = 46
ROOT_HIGH = 5
PART = 16
GROUPS_AT_ONCE = 2
VMEM = pl.BlockSpec(memory_space=pltpu.VMEM)
PARAMS = pltpu.CompilerParams(vmem_limit_bytes=32 * 1024 * 1024)


def tile_of(ref, chunk, group):
    return ref[pl.ds(pl.multiple_of(chunk * SUBLANES, SUBLANES), SUBLANES), group * LANES : (group + 1) * LANES]


def spread(tile, row):
    return jnp.broadcast_to(tile[row : row + 1], (SUBLANES, LANES))


def summary_kernel(key_hbm, value_hbm, gate_hbm, grad_hbm, rate_hbm, skip_hbm, out_ref, ahead_ref, behind_ref, skip_ref, key_ref, value_ref, gate_ref, grad_ref, rate_ref, mixed, slope, sems):
    block, width = key_ref.shape
    modes = rate_ref.shape[0]
    halves, groups = modes // SUBLANES, width // LANES
    pairs = ((rate_hbm, rate_ref), (key_hbm, key_ref), (value_hbm, value_ref), (grad_hbm, grad_ref), (gate_hbm, gate_ref), (skip_hbm, skip_ref))
    copies = [pltpu.make_async_copy(source, target, sems.at[at]) for at, (source, target) in enumerate(pairs)]
    for copy in copies:
        copy.start()
    copies[0].wait()
    steps = {}
    for half in range(halves):
        for group in range(groups):
            rate = jnp.exp(rate_ref[half * SUBLANES : (half + 1) * SUBLANES, group * LANES : (group + 1) * LANES])
            steps[half, group] = jnp.exp(-rate)
    copies[1].wait()
    copies[2].wait()
    mixed[...] = key_ref[...].astype(jnp.float32) * value_ref[...].astype(jnp.float32)
    copies[3].wait()
    copies[4].wait()
    slope[...] = grad_ref[...].astype(jnp.float32) * gate_ref[...].astype(jnp.float32)
    copies[5].wait()
    zero = jnp.zeros((SUBLANES, LANES), jnp.float32)
    for first in range(0, groups, GROUPS_AT_ONCE):
        held = range(first, first + GROUPS_AT_ONCE)
        keys = [(half, group) for half in range(halves) for group in held]

        def advance(part, carry):
            carry = list(carry)
            for at, (half, group) in enumerate(keys):
                rows = slice(half * SUBLANES, (half + 1) * SUBLANES)
                lanes = slice(group * LANES, (group + 1) * LANES)
                ahead_ref[part, rows, lanes] = carry[at][0]
                behind_ref[block // PART - 1 - part, rows, lanes] = carry[at][4]
            for piece in range(PART // SUBLANES):
                chunk = part * (PART // SUBLANES) + piece
                x_tiles = {group: tile_of(mixed, chunk, group) for group in held}
                z_tiles = {group: tile_of(slope, chunk, group) for group in held}
                back_tiles = {group: tile_of(slope, block // SUBLANES - 1 - chunk, group) for group in held}
                for inner in range(SUBLANES):
                    x_rows = {group: spread(x_tiles[group], inner) for group in held}
                    z_rows = {group: spread(z_tiles[group], inner) for group in held}
                    back_rows = {group: spread(back_tiles[group], SUBLANES - 1 - inner) for group in held}
                    for at, (half, group) in enumerate(keys):
                        state, timed, plain_sum, timed_sum, back, back_timed = carry[at]
                        step = steps[half, group]
                        moved = step * state
                        timed = step * timed + moved
                        state = moved + x_rows[group]
                        plain_sum = plain_sum + z_rows[group] * state
                        timed_sum = timed_sum + z_rows[group] * timed
                        back_moved = step * back
                        back_timed = step * back_timed + back_moved
                        back = back_moved + back_rows[group]
                        carry[at] = (state, timed, plain_sum, timed_sum, back, back_timed)
            return tuple(carry)

        done = lax.fori_loop(0, block // PART, advance, tuple((zero,) * 6 for _ in keys))
        for at, (half, group) in enumerate(keys):
            state, timed, plain_sum, timed_sum, back, back_timed = done[at]
            step = steps[half, group]
            base = (group * modes + half * SUBLANES) * ROWS_OUT
            lanes = slice(group * LANES, (group + 1) * LANES)
            skip_part = jnp.sum(mixed[:, lanes] * slope[:, lanes], axis=0, keepdims=True)
            rows = (
                step * state,
                step * (timed + state),
                back,
                back_timed,
                plain_sum,
                timed_sum,
                jnp.broadcast_to(skip_part, (SUBLANES, LANES)),
            )
            for row, value in enumerate(rows):
                out_ref[pl.ds(base + row, SUBLANES, stride=ROWS_OUT), :] = value


def shifted(value, amount):
    rows = lax.broadcasted_iota(jnp.int32, value.shape, 0)
    moved = pltpu.roll(value, amount % value.shape[0], 0)
    keep = rows >= amount if amount > 0 else rows < value.shape[0] + amount
    return jnp.where(keep, moved, 0.0)


def scan_kernel(block, modes, lead, in_ref, res_ref, rate_ref, out_ref):
    chunk = SUBLANES
    turn, cut = divmod(-lead % (chunk * SUBLANES), chunk)
    seam = lax.broadcasted_iota(jnp.int32, (SUBLANES, LANES), 0) == turn
    blocks = chunk * SUBLANES
    place = lax.rem(lax.axis_index("seq") + (blocks - lead), blocks)
    own_mode, own_group = lax.rem(place, modes), lax.div(place, modes)
    rows = lax.broadcasted_iota(jnp.int32, (modes, LANES), 0)

    def own(ref):
        picked = jnp.zeros((modes, LANES), jnp.float32)
        for group in range(ref.shape[1] // LANES):
            mine = rows == jnp.where(own_group == group, own_mode, -1)
            picked = jnp.where(mine, ref[:, group * LANES : (group + 1) * LANES], picked)
        return jnp.broadcast_to(jnp.sum(picked, axis=0, keepdims=True), (SUBLANES, LANES))

    rate = jnp.exp(own(rate_ref))
    unit = jnp.sqrt(2.0 * rate / modes)
    amplitude = own(res_ref) * unit
    power = [jnp.exp(-float(block * v) * rate) for v in range(chunk)]
    decay = power[1]

    def load(v, row):
        return in_ref[pl.ds(v * ROWS_OUT + row, SUBLANES, stride=chunk * ROWS_OUT), :]

    zero = jnp.zeros((SUBLANES, LANES), jnp.float32)
    state, timed, back = zero, zero, zero
    states, timeds, backs = [], [], [None] * chunk
    for v in range(chunk):
        if v == cut:
            state, timed = jnp.where(seam, 0.0, state), jnp.where(seam, 0.0, timed)
        states.append(state)
        timeds.append(timed)
        moved = decay * state
        timed = decay * timed + float(block) * moved + load(v, 1)
        state = moved + load(v, 0)
    for v in reversed(range(chunk)):
        backs[v] = back
        back = decay * back + load(v, 2)
        if v == cut:
            back = jnp.where(seam, 0.0, back)
    state, timed = (pltpu.roll(value, -turn % SUBLANES, 0) for value in (state, timed))
    back = pltpu.roll(back, (SUBLANES - 1 - turn) % SUBLANES, 0)
    span = block * chunk
    distance = 1
    while distance < SUBLANES:
        far = jnp.exp(-float(span * distance) * rate)
        older = far * shifted(state, distance)
        timed = timed + far * shifted(timed, distance) + float(span * distance) * older
        state = state + older
        back = back + far * shifted(back, -distance)
        distance *= 2
    state, timed = (pltpu.roll(value, (turn + 1) % SUBLANES, 0) for value in (state, timed))
    back = pltpu.roll(back, turn, 0)
    start_state, start_timed = jnp.where(seam, 0.0, state), jnp.where(seam, 0.0, timed)
    end_back = jnp.where(seam, 0.0, back)
    plain, slow, skip = zero, zero, zero
    for v in range(chunk):
        before, before_timed = (start_state, start_timed) if v >= cut else (state, timed)
        entering = states[v] + power[v] * before
        entering_timed = timeds[v] + power[v] * (before_timed + float(block * v) * before)
        leaving = backs[v] + power[chunk - 1 - v] * (back if v >= cut else end_back)
        slope, slope_timed = load(v, 2), load(v, 3)
        plain = plain + load(v, 4) + slope * entering
        slow = slow + load(v, 5) + slope_timed * entering + slope * entering_timed
        skip = skip + load(v, 6)
        for row, value in ((0, entering), (1, leaving)):
            out_ref[pl.ds(v * ROWS_BACK + row, SUBLANES, stride=chunk * ROWS_BACK), :] = value

    def total(value):
        return jnp.broadcast_to(jnp.sum(value, axis=0, keepdims=True), (SUBLANES, LANES))

    plain, slow, skip = total(plain), total(slow), total(skip)
    raw_res = plain * unit
    raw_log = (0.5 * plain - rate * slow) * amplitude
    for v in range(chunk):
        for row, value in ((2, raw_res), (3, raw_log), (4, skip)):
            out_ref[pl.ds(v * ROWS_BACK + row, SUBLANES, stride=chunk * ROWS_BACK), :] = value


def square_kernel(modes, in_ref, res_ref, log_ref, skip_ref, out_ref):
    groups = res_ref.shape[1] // LANES
    first = lax.broadcasted_iota(jnp.int32, (SUBLANES, LANES), 0) == 0
    total = jnp.zeros((SUBLANES, LANES), jnp.float32)
    for group in range(groups):
        lanes = slice(group * LANES, (group + 1) * LANES)
        for half in range(modes // SUBLANES):
            base = (group * modes + half * SUBLANES) * ROWS_BACK
            for row, ref in ((2, res_ref), (3, log_ref)):
                value = in_ref[pl.ds(base + row, SUBLANES, stride=ROWS_BACK), :]
                ref[half * SUBLANES : (half + 1) * SUBLANES, lanes] = value
                total = total + value * value
        skip = in_ref[pl.ds(group * modes * ROWS_BACK + 4, 1), :]
        skip_ref[:, lanes] = skip
        total = total + jnp.where(first, skip * skip, 0.0)
    out_ref[...] = jnp.broadcast_to(jnp.sum(total, axis=0, keepdims=True), out_ref.shape)


def output_kernel(count, in_ref, squares_ref, raw_res_ref, raw_log_ref, raw_skip_ref, ahead_ref, behind_ref, key_ref, value_ref, gate_ref, grad_ref, res_ref, rate_ref, skip_ref, out_hbm, gate_hbm, key_hbm, value_hbm, res_hbm, log_hbm, gain_hbm, out_ref, gate_out, key_out, value_out, mixed, slope, entering, leaving, taps, res_out, log_out, gain_out, sems, clip_sems):
    block, width = key_ref.shape
    modes = rate_ref.shape[0]
    groups = width // LANES
    parts, halves = block // PART, modes // SUBLANES
    tile = (SUBLANES, LANES)
    zero = jnp.zeros(tile, jnp.float32)
    place = lax.broadcasted_iota(jnp.int32, tile, 0)
    odd, second, fourth = ((place & bit) != 0 for bit in (1, 2, 4))

    def row(ref, at):
        return jnp.broadcast_to(ref[at : at + 1, :], tile)

    squares = jnp.sum(jnp.sum(squares_ref[...], axis=0, keepdims=True), axis=1, keepdims=True)
    factor = CLIP_RMS / jnp.maximum(jnp.sqrt(squares / count), CLIP_RMS)
    copies = []
    for at, (raw, held, target) in enumerate(
        ((raw_res_ref, res_out, res_hbm), (raw_log_ref, log_out, log_hbm), (raw_skip_ref, gain_out, gain_hbm))
    ):
        held[...] = raw[...] * factor
        copies.append(pltpu.make_async_copy(held, target, clip_sems.at[at]))
        copies[-1].start()

    def leave(group, first, *pairs):
        lanes = slice(group * LANES, (group + 1) * LANES)
        for at, (source, target) in enumerate(pairs):
            copies.append(pltpu.make_async_copy(source.at[:, lanes], target.at[:, lanes], sems.at[group, first + at]))
            copies[-1].start()

    for group in range(groups):
        lanes = slice(group * LANES, (group + 1) * LANES)
        for part in range(parts):
            at, rows = part * (PART + SUBLANES), slice(part * PART, (part + 1) * PART)
            for ref in (mixed, slope):
                ref[at : at + SUBLANES, :] = zero
            start = at + SUBLANES
            mixed[start : start + PART, :] = key_ref[rows, lanes].astype(jnp.float32) * value_ref[rows, lanes].astype(jnp.float32)
            slope[start : start + PART, :] = grad_ref[rows, lanes].astype(jnp.float32) * gate_ref[rows, lanes].astype(jnp.float32)
        for ref in (mixed, slope):
            ref[parts * (PART + SUBLANES) :, :] = zero
        powers = []
        for half in range(halves):
            rows = slice(half * SUBLANES, (half + 1) * SUBLANES)
            rate = jnp.exp(rate_ref[rows, lanes])
            amplitude = res_ref[rows, lanes] * jnp.sqrt(2.0 * rate / modes)
            step, leap = jnp.exp(-rate), jnp.exp(-float(PART) * rate)
            square = step * step
            powers.append((amplitude, step, square, square * square, jnp.exp(-float(SUBLANES) * rate)))
            base = (group * modes + half * SUBLANES) * ROWS_BACK
            wave = in_ref[pl.ds(base, SUBLANES, stride=ROWS_BACK), :]
            echo = in_ref[pl.ds(base + 1, SUBLANES, stride=ROWS_BACK), :]
            for part in range(parts):
                mirror = parts - 1 - part
                at, mirrored = part * modes + half * SUBLANES, mirror * modes + half * SUBLANES
                entering[at : at + SUBLANES, :] = amplitude * (step * ahead_ref[part, rows, lanes] + wave)
                leaving[mirrored : mirrored + SUBLANES, :] = amplitude * (behind_ref[mirror, rows, lanes] + echo)
                if part + 1 < parts:
                    wave, echo = wave * leap, echo * leap
        ahead, back = [zero] * (2 * parts), [zero] * (2 * parts)
        near, far = zero, zero
        for mode in range(modes):
            half, inner = divmod(mode, SUBLANES)
            amplitude, step, square, fourth_power, jump = (spread(power, inner) for power in powers[half])
            up = jnp.where(odd, step, 1.0) * jnp.where(second, square, 1.0) * jnp.where(fourth, fourth_power, 1.0)
            down = step * jnp.where(odd, 1.0, step) * jnp.where(second, 1.0, square) * jnp.where(fourth, 1.0, fourth_power)
            tap = amplitude * up
            near, far = near + tap, far + tap * jump
            for part in range(parts):
                wave = row(entering, part * modes + mode) * up
                echo = row(leaving, part * modes + mode) * down
                ahead[2 * part] = ahead[2 * part] + wave
                ahead[2 * part + 1] = ahead[2 * part + 1] + wave * jump
                back[2 * part + 1] = back[2 * part + 1] + echo
                back[2 * part] = back[2 * part] + echo * jump
        taps[0:SUBLANES, :] = near
        taps[SUBLANES:, :] = far
        skip_row = jnp.broadcast_to(skip_ref[:, lanes], tile)
        for shift in range(SUBLANES):
            close, apart = row(taps, shift), row(taps, SUBLANES + shift)
            if shift == 0:
                close = close + skip_row
            for part in range(parts):
                start = part * (PART + SUBLANES) + SUBLANES
                low = mixed[pl.ds(start - shift, SUBLANES), :]
                high = mixed[pl.ds(start + SUBLANES - shift, SUBLANES), :]
                ahead[2 * part] = ahead[2 * part] + close * low
                ahead[2 * part + 1] = ahead[2 * part + 1] + (close * high + apart * low)
        for pair in range(parts):
            rows = slice(pair * PART, (pair + 1) * PART)
            filtered = jnp.concatenate([ahead[2 * pair], ahead[2 * pair + 1]], axis=0)
            out_ref[rows, lanes] = (gate_ref[rows, lanes].astype(jnp.float32) * filtered).astype(jnp.bfloat16)
            gate_out[rows, lanes] = (grad_ref[rows, lanes].astype(jnp.float32) * filtered).astype(jnp.bfloat16)
        leave(group, 0, (out_ref, out_hbm), (gate_out, gate_hbm))
        for shift in range(SUBLANES):
            close, apart = row(taps, shift), row(taps, SUBLANES + shift)
            if shift == 0:
                close = close + skip_row
            for part in range(parts):
                start = part * (PART + SUBLANES) + SUBLANES
                low = slope[pl.ds(start + shift, SUBLANES), :]
                high = slope[pl.ds(start + SUBLANES + shift, SUBLANES), :]
                back[2 * part] = back[2 * part] + (close * low + apart * high)
                back[2 * part + 1] = back[2 * part + 1] + close * high
        for pair in range(parts):
            rows = slice(pair * PART, (pair + 1) * PART)
            mixed_grad = jnp.concatenate([back[2 * pair], back[2 * pair + 1]], axis=0)
            key_out[rows, lanes] = (value_ref[rows, lanes].astype(jnp.float32) * mixed_grad).astype(jnp.bfloat16)
            value_out[rows, lanes] = (key_ref[rows, lanes].astype(jnp.float32) * mixed_grad).astype(jnp.bfloat16)
        leave(group, 2, (key_out, key_hbm), (value_out, value_hbm))
    for copy in copies:
        copy.wait()


def in_hbm(*arrays):
    return tuple(pltpu.with_memory_space_constraint(array, pltpu.HBM) for array in arrays)


def call(kernel, out_shape, *args, scratch=(), space=VMEM, out_space=VMEM):
    multiple = isinstance(out_shape, (tuple, list))
    return pl.pallas_call(
        kernel,
        out_shape=out_shape,
        in_specs=[space] * len(args),
        out_specs=[out_space] * len(out_shape) if multiple else out_space,
        scratch_shapes=list(scratch),
        compiler_params=PARAMS,
    )(*args)


def exchange(rows, axis, groups=None):
    count, lanes = rows.shape
    moved = lax.all_to_all(rows.reshape(count, 1, lanes), axis, 0, 0, axis_index_groups=groups, tiled=True)
    return moved.reshape(count, lanes)


def near_groups(blocks, shards):
    run = blocks // Y_RUN
    groups = []
    for device in range(blocks):
        other = device ^ (2 * run)
        members = [(other if shard % 2 else device) * shards + shard for shard in range(shards)]
        groups.append(members[ROOT_HIGH:] + members[:ROOT_HIGH])
    return groups


def floats(*shape):
    return jax.ShapeDtypeStruct(shape, jnp.float32)


def summarize(key_in, value_in, gate_in, out_grad, log_rate, skip):
    block, width = key_in.shape
    modes = log_rate.shape[0]
    return call(
        summary_kernel,
        (
            floats(modes * (width // LANES) * ROWS_OUT, LANES),
            floats(block // PART, modes, width),
            floats(block // PART, modes, width),
            floats(1, width),
        ),
        *in_hbm(key_in, value_in, gate_in, out_grad, log_rate, skip),
        scratch=[pltpu.VMEM((block, width), jnp.bfloat16)] * 4
        + [pltpu.VMEM((modes, width), jnp.float32)]
        + [pltpu.VMEM((block, width), jnp.float32)] * 2
        + [pltpu.SemaphoreType.DMA((6,))],
        space=pl.BlockSpec(memory_space=pltpu.HBM),
    )


def finish(states, squares, raw_res, raw_log, raw_skip, ahead, behind, key_in, value_in, gate_in, out_grad, residue, log_rate, skip_row):
    block, width = key_in.shape
    modes, groups, shards = residue.shape[0], width // LANES, squares.shape[0]
    return call(
        functools.partial(output_kernel, float((2 * modes + 1) * width * shards)),
        (jax.ShapeDtypeStruct((block, width), jnp.bfloat16),) * 4 + (floats(modes, width), floats(modes, width), floats(1, width)),
        states, squares, raw_res, raw_log, raw_skip, ahead, behind, key_in, value_in, gate_in, out_grad, residue, log_rate, skip_row,
        out_space=pl.BlockSpec(memory_space=pl.ANY),
        scratch=[pltpu.VMEM((block, width), jnp.bfloat16)] * 4
        + [pltpu.VMEM((block // PART * (PART + SUBLANES) + SUBLANES, LANES), jnp.float32)] * 2
        + [pltpu.VMEM((block // PART * modes, LANES), jnp.float32)] * 2
        + [pltpu.VMEM((PART, LANES), jnp.float32)]
        + [pltpu.VMEM((modes, width), jnp.float32)] * 2
        + [pltpu.VMEM((1, width), jnp.float32), pltpu.SemaphoreType.DMA((groups, 4)), pltpu.SemaphoreType.DMA((3,))],
    )


def per_device(gate_in, key_in, value_in, out_grad, residue, log_rate, skip):
    block, width = gate_in.shape
    modes = residue.shape[0]
    blocks = lax.axis_size("seq")
    shards = lax.axis_size("chan")
    groups = width // LANES
    owners = groups * modes
    assert owners == blocks
    order = [(LEAD + at) % blocks for at in range(blocks)]

    sent, ahead, behind, skip_row = summarize(key_in, value_in, gate_in, out_grad, log_rate, skip.reshape(1, width))
    arrived = exchange(sent, "seq", [order])
    reply = call(
        functools.partial(scan_kernel, block, modes, LEAD),
        floats(blocks * ROWS_BACK, LANES),
        arrived, residue, log_rate,
    )
    states = exchange(reply, "seq", [order])
    raw_res, raw_log, raw_skip, squares = call(
        functools.partial(square_kernel, modes),
        (floats(modes, width), floats(modes, width), floats(1, width), floats(shards, LANES)),
        states,
    )
    squares = exchange(squares, ("seq", "chan"), near_groups(blocks, shards))
    gated_out, gate_grad, key_grad, value_grad, residue_grad, log_rate_grad, skip_grad = finish(
        states, squares, raw_res, raw_log, raw_skip, ahead, behind, key_in, value_in, gate_in, out_grad, residue, log_rate, skip_row
    )
    return gated_out, gate_grad, key_grad, value_grad, residue_grad, log_rate_grad, skip_grad.reshape(width)


def solution(mesh):
    field, parameter, gain = P("seq", "chan"), P(None, "chan"), P("chan")
    return jax.shard_map(
        per_device,
        mesh=mesh,
        in_specs=(field, field, field, field, parameter, parameter, gain),
        out_specs=(field, field, field, field, parameter, parameter, gain),
        check_vma=False,
    )
```

```python
import functools

import jax
import jax.numpy as jnp
from jax import lax
from jax.experimental import pallas as pl
from jax.experimental.pallas import tpu as pltpu
from jax.sharding import PartitionSpec as P

CLIP_RMS = 1.0
LANES = 128
SUBLANES = 8
ROWS_OUT = 7
ROWS_BACK = 5
Y_RUN = 4
LEADS = (47, 31)
ROOT_HIGH = 5
PART = 16
GROUPS_AT_ONCE = 2
VMEM = pl.BlockSpec(memory_space=pltpu.VMEM)
PARAMS = pltpu.CompilerParams(vmem_limit_bytes=32 * 1024 * 1024)


def tile_of(ref, chunk, group):
    return ref[pl.ds(pl.multiple_of(chunk * SUBLANES, SUBLANES), SUBLANES), group * LANES : (group + 1) * LANES]


def spread(tile, row):
    return jnp.broadcast_to(tile[row : row + 1], (SUBLANES, LANES))


def summary_kernel(key_hbm, value_hbm, gate_hbm, grad_hbm, rate_hbm, skip_hbm, out_ref, ahead_ref, behind_ref, skip_ref, key_ref, value_ref, gate_ref, grad_ref, rate_ref, mixed, slope, sems):
    block, width = key_ref.shape
    modes = rate_ref.shape[0]
    halves, groups = modes // SUBLANES, width // LANES
    pairs = ((rate_hbm, rate_ref), (key_hbm, key_ref), (value_hbm, value_ref), (grad_hbm, grad_ref), (gate_hbm, gate_ref), (skip_hbm, skip_ref))
    copies = [pltpu.make_async_copy(source, target, sems.at[at]) for at, (source, target) in enumerate(pairs)]
    for copy in copies:
        copy.start()
    copies[0].wait()
    steps = {}
    for half in range(halves):
        for group in range(groups):
            rate = jnp.exp(rate_ref[half * SUBLANES : (half + 1) * SUBLANES, group * LANES : (group + 1) * LANES])
            steps[half, group] = jnp.exp(-rate)
    copies[1].wait()
    copies[2].wait()
    mixed[...] = key_ref[...].astype(jnp.float32) * value_ref[...].astype(jnp.float32)
    copies[3].wait()
    copies[4].wait()
    slope[...] = grad_ref[...].astype(jnp.float32) * gate_ref[...].astype(jnp.float32)
    copies[5].wait()
    zero = jnp.zeros((SUBLANES, LANES), jnp.float32)
    for first in range(0, groups, GROUPS_AT_ONCE):
        held = range(first, first + GROUPS_AT_ONCE)
        keys = [(half, group) for half in range(halves) for group in held]

        def advance(part, carry):
            carry = list(carry)
            for at, (half, group) in enumerate(keys):
                rows = slice(half * SUBLANES, (half + 1) * SUBLANES)
                lanes = slice(group * LANES, (group + 1) * LANES)
                ahead_ref[part, rows, lanes] = carry[at][0]
                behind_ref[block // PART - 1 - part, rows, lanes] = carry[at][4]
            for piece in range(PART // SUBLANES):
                chunk = part * (PART // SUBLANES) + piece
                x_tiles = {group: tile_of(mixed, chunk, group) for group in held}
                z_tiles = {group: tile_of(slope, chunk, group) for group in held}
                back_tiles = {group: tile_of(slope, block // SUBLANES - 1 - chunk, group) for group in held}
                for inner in range(SUBLANES):
                    x_rows = {group: spread(x_tiles[group], inner) for group in held}
                    z_rows = {group: spread(z_tiles[group], inner) for group in held}
                    back_rows = {group: spread(back_tiles[group], SUBLANES - 1 - inner) for group in held}
                    for at, (half, group) in enumerate(keys):
                        state, timed, plain_sum, timed_sum, back, back_timed = carry[at]
                        step = steps[half, group]
                        moved = step * state
                        timed = step * timed + moved
                        state = moved + x_rows[group]
                        plain_sum = plain_sum + z_rows[group] * state
                        timed_sum = timed_sum + z_rows[group] * timed
                        back_moved = step * back
                        back_timed = step * back_timed + back_moved
                        back = back_moved + back_rows[group]
                        carry[at] = (state, timed, plain_sum, timed_sum, back, back_timed)
            return tuple(carry)

        done = lax.fori_loop(0, block // PART, advance, tuple((zero,) * 6 for _ in keys))
        for at, (half, group) in enumerate(keys):
            state, timed, plain_sum, timed_sum, back, back_timed = done[at]
            step = steps[half, group]
            base = (group * modes + half * SUBLANES) * ROWS_OUT
            lanes = slice(group * LANES, (group + 1) * LANES)
            skip_part = jnp.sum(mixed[:, lanes] * slope[:, lanes], axis=0, keepdims=True)
            rows = (
                step * state,
                step * (timed + state),
                back,
                back_timed,
                plain_sum,
                timed_sum,
                jnp.broadcast_to(skip_part, (SUBLANES, LANES)),
            )
            for row, value in enumerate(rows):
                out_ref[pl.ds(base + row, SUBLANES, stride=ROWS_OUT), :] = value


def shifted(value, amount):
    rows = lax.broadcasted_iota(jnp.int32, value.shape, 0)
    moved = pltpu.roll(value, amount % value.shape[0], 0)
    keep = rows >= amount if amount > 0 else rows < value.shape[0] + amount
    return jnp.where(keep, moved, 0.0)


def scan_kernel(block, modes, in_ref, res_ref, rate_ref, out_ref):
    chunk = SUBLANES
    blocks = chunk * SUBLANES
    upper = lax.rem(lax.axis_index("chan"), 2)
    (low_turn, cut), (high_turn, _) = (divmod(-lead % blocks, chunk) for lead in LEADS)
    turn = jnp.where(upper == 1, high_turn, low_turn)
    lead = jnp.where(upper == 1, LEADS[1], LEADS[0])
    seam = lax.broadcasted_iota(jnp.int32, (SUBLANES, LANES), 0) == turn
    place = lax.rem(lax.axis_index("seq") + (blocks - lead), blocks)
    own_mode, own_group = lax.rem(place, modes), lax.div(place, modes)
    rows = lax.broadcasted_iota(jnp.int32, (modes, LANES), 0)

    def own(ref):
        picked = jnp.zeros((modes, LANES), jnp.float32)
        for group in range(ref.shape[1] // LANES):
            mine = rows == jnp.where(own_group == group, own_mode, -1)
            picked = jnp.where(mine, ref[:, group * LANES : (group + 1) * LANES], picked)
        return jnp.broadcast_to(jnp.sum(picked, axis=0, keepdims=True), (SUBLANES, LANES))

    rate = jnp.exp(own(rate_ref))
    unit = jnp.sqrt(2.0 * rate / modes)
    amplitude = own(res_ref) * unit
    power = [jnp.exp(-float(block * v) * rate) for v in range(chunk)]
    decay = power[1]

    def load(v, row):
        return in_ref[pl.ds(v * ROWS_OUT + row, SUBLANES, stride=chunk * ROWS_OUT), :]

    zero = jnp.zeros((SUBLANES, LANES), jnp.float32)
    state, timed, back = zero, zero, zero
    states, timeds, backs = [], [], [None] * chunk
    for v in range(chunk):
        if v == cut:
            state, timed = jnp.where(seam, 0.0, state), jnp.where(seam, 0.0, timed)
        states.append(state)
        timeds.append(timed)
        moved = decay * state
        timed = decay * timed + float(block) * moved + load(v, 1)
        state = moved + load(v, 0)
    for v in reversed(range(chunk)):
        backs[v] = back
        back = decay * back + load(v, 2)
        if v == cut:
            back = jnp.where(seam, 0.0, back)
    state, timed = (pltpu.roll(value, SUBLANES - turn, 0) for value in (state, timed))
    back = pltpu.roll(back, SUBLANES - 1 - turn, 0)
    span = block * chunk
    distance = 1
    while distance < SUBLANES:
        far = jnp.exp(-float(span * distance) * rate)
        older = far * shifted(state, distance)
        timed = timed + far * shifted(timed, distance) + float(span * distance) * older
        state = state + older
        back = back + far * shifted(back, -distance)
        distance *= 2
    state, timed = (pltpu.roll(value, turn + 1, 0) for value in (state, timed))
    back = pltpu.roll(back, turn, 0)
    start_state, start_timed = jnp.where(seam, 0.0, state), jnp.where(seam, 0.0, timed)
    end_back = jnp.where(seam, 0.0, back)
    plain, slow, skip = zero, zero, zero
    for v in range(chunk):
        before, before_timed = (start_state, start_timed) if v >= cut else (state, timed)
        entering = states[v] + power[v] * before
        entering_timed = timeds[v] + power[v] * (before_timed + float(block * v) * before)
        leaving = backs[v] + power[chunk - 1 - v] * (back if v >= cut else end_back)
        slope, slope_timed = load(v, 2), load(v, 3)
        plain = plain + load(v, 4) + slope * entering
        slow = slow + load(v, 5) + slope_timed * entering + slope * entering_timed
        skip = skip + load(v, 6)
        for row, value in ((0, entering), (1, leaving)):
            out_ref[pl.ds(v * ROWS_BACK + row, SUBLANES, stride=chunk * ROWS_BACK), :] = value

    def total(value):
        return jnp.broadcast_to(jnp.sum(value, axis=0, keepdims=True), (SUBLANES, LANES))

    plain, slow, skip = total(plain), total(slow), total(skip)
    raw_res = plain * unit
    raw_log = (0.5 * plain - rate * slow) * amplitude
    for v in range(chunk):
        for row, value in ((2, raw_res), (3, raw_log), (4, skip)):
            out_ref[pl.ds(v * ROWS_BACK + row, SUBLANES, stride=chunk * ROWS_BACK), :] = value


def square_kernel(modes, in_ref, res_ref, log_ref, skip_ref, out_ref):
    groups = res_ref.shape[1] // LANES
    first = lax.broadcasted_iota(jnp.int32, (SUBLANES, LANES), 0) == 0
    total = jnp.zeros((SUBLANES, LANES), jnp.float32)
    for group in range(groups):
        lanes = slice(group * LANES, (group + 1) * LANES)
        for half in range(modes // SUBLANES):
            base = (group * modes + half * SUBLANES) * ROWS_BACK
            for row, ref in ((2, res_ref), (3, log_ref)):
                value = in_ref[pl.ds(base + row, SUBLANES, stride=ROWS_BACK), :]
                ref[half * SUBLANES : (half + 1) * SUBLANES, lanes] = value
                total = total + value * value
        skip = in_ref[pl.ds(group * modes * ROWS_BACK + 4, 1), :]
        skip_ref[:, lanes] = skip
        total = total + jnp.where(first, skip * skip, 0.0)
    out_ref[...] = jnp.broadcast_to(jnp.sum(total, axis=0, keepdims=True), out_ref.shape)


def output_kernel(count, in_ref, squares_ref, raw_res_ref, raw_log_ref, raw_skip_ref, ahead_ref, behind_ref, key_ref, value_ref, gate_ref, grad_ref, res_ref, rate_ref, skip_ref, out_hbm, gate_hbm, key_hbm, value_hbm, res_hbm, log_hbm, gain_hbm, out_ref, gate_out, key_out, value_out, mixed, slope, entering, leaving, taps, res_out, log_out, gain_out, sems, clip_sems):
    block, width = key_ref.shape
    modes = rate_ref.shape[0]
    groups = width // LANES
    parts, halves = block // PART, modes // SUBLANES
    tile = (SUBLANES, LANES)
    zero = jnp.zeros(tile, jnp.float32)
    place = lax.broadcasted_iota(jnp.int32, tile, 0)
    odd, second, fourth = ((place & bit) != 0 for bit in (1, 2, 4))

    def row(ref, at):
        return jnp.broadcast_to(ref[at : at + 1, :], tile)

    squares = jnp.sum(jnp.sum(squares_ref[...], axis=0, keepdims=True), axis=1, keepdims=True)
    factor = CLIP_RMS / jnp.maximum(jnp.sqrt(squares / count), CLIP_RMS)
    copies = []
    for at, (raw, held, target) in enumerate(
        ((raw_res_ref, res_out, res_hbm), (raw_log_ref, log_out, log_hbm), (raw_skip_ref, gain_out, gain_hbm))
    ):
        held[...] = raw[...] * factor
        copies.append(pltpu.make_async_copy(held, target, clip_sems.at[at]))
        copies[-1].start()

    def leave(group, first, *pairs):
        lanes = slice(group * LANES, (group + 1) * LANES)
        for at, (source, target) in enumerate(pairs):
            copies.append(pltpu.make_async_copy(source.at[:, lanes], target.at[:, lanes], sems.at[group, first + at]))
            copies[-1].start()

    for group in range(groups):
        lanes = slice(group * LANES, (group + 1) * LANES)
        for part in range(parts):
            at, rows = part * (PART + SUBLANES), slice(part * PART, (part + 1) * PART)
            for ref in (mixed, slope):
                ref[at : at + SUBLANES, :] = zero
            start = at + SUBLANES
            mixed[start : start + PART, :] = key_ref[rows, lanes].astype(jnp.float32) * value_ref[rows, lanes].astype(jnp.float32)
            slope[start : start + PART, :] = grad_ref[rows, lanes].astype(jnp.float32) * gate_ref[rows, lanes].astype(jnp.float32)
        for ref in (mixed, slope):
            ref[parts * (PART + SUBLANES) :, :] = zero
        powers = []
        for half in range(halves):
            rows = slice(half * SUBLANES, (half + 1) * SUBLANES)
            rate = jnp.exp(rate_ref[rows, lanes])
            amplitude = res_ref[rows, lanes] * jnp.sqrt(2.0 * rate / modes)
            step, leap = jnp.exp(-rate), jnp.exp(-float(PART) * rate)
            square = step * step
            powers.append((amplitude, step, square, square * square, jnp.exp(-float(SUBLANES) * rate)))
            base = (group * modes + half * SUBLANES) * ROWS_BACK
            wave = in_ref[pl.ds(base, SUBLANES, stride=ROWS_BACK), :]
            echo = in_ref[pl.ds(base + 1, SUBLANES, stride=ROWS_BACK), :]
            for part in range(parts):
                mirror = parts - 1 - part
                at, mirrored = part * modes + half * SUBLANES, mirror * modes + half * SUBLANES
                entering[at : at + SUBLANES, :] = amplitude * (step * ahead_ref[part, rows, lanes] + wave)
                leaving[mirrored : mirrored + SUBLANES, :] = amplitude * (behind_ref[mirror, rows, lanes] + echo)
                if part + 1 < parts:
                    wave, echo = wave * leap, echo * leap
        ahead, back = [zero] * (2 * parts), [zero] * (2 * parts)
        near, far = zero, zero
        for mode in range(modes):
            half, inner = divmod(mode, SUBLANES)
            amplitude, step, square, fourth_power, jump = (spread(power, inner) for power in powers[half])
            up = jnp.where(odd, step, 1.0) * jnp.where(second, square, 1.0) * jnp.where(fourth, fourth_power, 1.0)
            down = step * jnp.where(odd, 1.0, step) * jnp.where(second, 1.0, square) * jnp.where(fourth, 1.0, fourth_power)
            tap = amplitude * up
            near, far = near + tap, far + tap * jump
            for part in range(parts):
                wave = row(entering, part * modes + mode) * up
                echo = row(leaving, part * modes + mode) * down
                ahead[2 * part] = ahead[2 * part] + wave
                ahead[2 * part + 1] = ahead[2 * part + 1] + wave * jump
                back[2 * part + 1] = back[2 * part + 1] + echo
                back[2 * part] = back[2 * part] + echo * jump
        taps[0:SUBLANES, :] = near
        taps[SUBLANES:, :] = far
        skip_row = jnp.broadcast_to(skip_ref[:, lanes], tile)
        for shift in range(SUBLANES):
            close, apart = row(taps, shift), row(taps, SUBLANES + shift)
            if shift == 0:
                close = close + skip_row
            for part in range(parts):
                start = part * (PART + SUBLANES) + SUBLANES
                low = mixed[pl.ds(start - shift, SUBLANES), :]
                high = mixed[pl.ds(start + SUBLANES - shift, SUBLANES), :]
                ahead[2 * part] = ahead[2 * part] + close * low
                ahead[2 * part + 1] = ahead[2 * part + 1] + (close * high + apart * low)
        for pair in range(parts):
            rows = slice(pair * PART, (pair + 1) * PART)
            filtered = jnp.concatenate([ahead[2 * pair], ahead[2 * pair + 1]], axis=0)
            out_ref[rows, lanes] = (gate_ref[rows, lanes].astype(jnp.float32) * filtered).astype(jnp.bfloat16)
            gate_out[rows, lanes] = (grad_ref[rows, lanes].astype(jnp.float32) * filtered).astype(jnp.bfloat16)
        leave(group, 0, (out_ref, out_hbm), (gate_out, gate_hbm))
        for shift in range(SUBLANES):
            close, apart = row(taps, shift), row(taps, SUBLANES + shift)
            if shift == 0:
                close = close + skip_row
            for part in range(parts):
                start = part * (PART + SUBLANES) + SUBLANES
                low = slope[pl.ds(start + shift, SUBLANES), :]
                high = slope[pl.ds(start + SUBLANES + shift, SUBLANES), :]
                back[2 * part] = back[2 * part] + (close * low + apart * high)
                back[2 * part + 1] = back[2 * part + 1] + close * high
        for pair in range(parts):
            rows = slice(pair * PART, (pair + 1) * PART)
            mixed_grad = jnp.concatenate([back[2 * pair], back[2 * pair + 1]], axis=0)
            key_out[rows, lanes] = (value_ref[rows, lanes].astype(jnp.float32) * mixed_grad).astype(jnp.bfloat16)
            value_out[rows, lanes] = (key_ref[rows, lanes].astype(jnp.float32) * mixed_grad).astype(jnp.bfloat16)
        leave(group, 2, (key_out, key_hbm), (value_out, value_hbm))
    for copy in copies:
        copy.wait()


def in_hbm(*arrays):
    return tuple(pltpu.with_memory_space_constraint(array, pltpu.HBM) for array in arrays)


def call(kernel, out_shape, *args, scratch=(), space=VMEM, out_space=VMEM):
    multiple = isinstance(out_shape, (tuple, list))
    return pl.pallas_call(
        kernel,
        out_shape=out_shape,
        in_specs=[space] * len(args),
        out_specs=[out_space] * len(out_shape) if multiple else out_space,
        scratch_shapes=list(scratch),
        compiler_params=PARAMS,
    )(*args)


def exchange(rows, axis, groups=None):
    count, lanes = rows.shape
    moved = lax.all_to_all(rows.reshape(count, 1, lanes), axis, 0, 0, axis_index_groups=groups, tiled=True)
    return moved.reshape(count, lanes)


def near_groups(blocks, shards):
    run = blocks // Y_RUN
    groups = []
    for device in range(blocks):
        other = device ^ (2 * run)
        members = [(other if shard % 2 else device) * shards + shard for shard in range(shards)]
        groups.append(members[ROOT_HIGH:] + members[:ROOT_HIGH])
    return groups


def floats(*shape):
    return jax.ShapeDtypeStruct(shape, jnp.float32)


def summarize(key_in, value_in, gate_in, out_grad, log_rate, skip):
    block, width = key_in.shape
    modes = log_rate.shape[0]
    return call(
        summary_kernel,
        (
            floats(modes * (width // LANES) * ROWS_OUT, LANES),
            floats(block // PART, modes, width),
            floats(block // PART, modes, width),
            floats(1, width),
        ),
        *in_hbm(key_in, value_in, gate_in, out_grad, log_rate, skip),
        scratch=[pltpu.VMEM((block, width), jnp.bfloat16)] * 4
        + [pltpu.VMEM((modes, width), jnp.float32)]
        + [pltpu.VMEM((block, width), jnp.float32)] * 2
        + [pltpu.SemaphoreType.DMA((6,))],
        space=pl.BlockSpec(memory_space=pltpu.HBM),
    )


def finish(states, squares, raw_res, raw_log, raw_skip, ahead, behind, key_in, value_in, gate_in, out_grad, residue, log_rate, skip_row):
    block, width = key_in.shape
    modes, groups, shards = residue.shape[0], width // LANES, squares.shape[0]
    return call(
        functools.partial(output_kernel, float((2 * modes + 1) * width * shards)),
        (jax.ShapeDtypeStruct((block, width), jnp.bfloat16),) * 4 + (floats(modes, width), floats(modes, width), floats(1, width)),
        states, squares, raw_res, raw_log, raw_skip, ahead, behind, key_in, value_in, gate_in, out_grad, residue, log_rate, skip_row,
        out_space=pl.BlockSpec(memory_space=pl.ANY),
        scratch=[pltpu.VMEM((block, width), jnp.bfloat16)] * 4
        + [pltpu.VMEM((block // PART * (PART + SUBLANES) + SUBLANES, LANES), jnp.float32)] * 2
        + [pltpu.VMEM((block // PART * modes, LANES), jnp.float32)] * 2
        + [pltpu.VMEM((PART, LANES), jnp.float32)]
        + [pltpu.VMEM((modes, width), jnp.float32)] * 2
        + [pltpu.VMEM((1, width), jnp.float32), pltpu.SemaphoreType.DMA((groups, 4)), pltpu.SemaphoreType.DMA((3,))],
    )


def per_device(gate_in, key_in, value_in, out_grad, residue, log_rate, skip):
    block, width = gate_in.shape
    modes = residue.shape[0]
    blocks = lax.axis_size("seq")
    shards = lax.axis_size("chan")
    groups = width // LANES
    owners = groups * modes
    assert owners == blocks
    orders = [[(LEADS[shard % 2] + at) % blocks * shards + shard for at in range(blocks)] for shard in range(shards)]
    sent, ahead, behind, skip_row = summarize(key_in, value_in, gate_in, out_grad, log_rate, skip.reshape(1, width))
    arrived = exchange(sent, ("seq", "chan"), orders)
    reply = call(
        functools.partial(scan_kernel, block, modes),
        floats(blocks * ROWS_BACK, LANES),
        arrived, residue, log_rate,
    )
    states = exchange(reply, ("seq", "chan"), orders)
    raw_res, raw_log, raw_skip, squares = call(
        functools.partial(square_kernel, modes),
        (floats(modes, width), floats(modes, width), floats(1, width), floats(shards, LANES)),
        states,
    )
    squares = exchange(squares, ("seq", "chan"), near_groups(blocks, shards))
    gated_out, gate_grad, key_grad, value_grad, residue_grad, log_rate_grad, skip_grad = finish(
        states, squares, raw_res, raw_log, raw_skip, ahead, behind, key_in, value_in, gate_in, out_grad, residue, log_rate, skip_row
    )
    return gated_out, gate_grad, key_grad, value_grad, residue_grad, log_rate_grad, skip_grad.reshape(width)


def solution(mesh):
    field, parameter, gain = P("seq", "chan"), P(None, "chan"), P("chan")
    return jax.shard_map(
        per_device,
        mesh=mesh,
        in_specs=(field, field, field, field, parameter, parameter, gain),
        out_specs=(field, field, field, field, parameter, parameter, gain),
        check_vma=False,
    )
```

```python
import functools

import jax
import jax.numpy as jnp
from jax import lax
from jax.experimental import pallas as pl
from jax.experimental.pallas import tpu as pltpu
from jax.sharding import PartitionSpec as P

CLIP_RMS = 1.0
LANES = 128
SUBLANES = 8
ROWS_OUT = 7
ROWS_BACK = 5
Y_RUN = 4
LEADS = (47, 31)
ROOT_HIGH = 5
PART = 16
GROUPS_AT_ONCE = 2
VMEM = pl.BlockSpec(memory_space=pltpu.VMEM)
PARAMS = pltpu.CompilerParams(vmem_limit_bytes=32 * 1024 * 1024)


def tile_of(ref, part, piece, group):
    row = part * (PART + SUBLANES) + (piece + 1) * SUBLANES
    return ref[group, pl.ds(pl.multiple_of(row, SUBLANES), SUBLANES), :]


def spread(tile, row):
    return jnp.broadcast_to(tile[row : row + 1], (SUBLANES, LANES))


def summary_kernel(key_hbm, value_hbm, gate_hbm, grad_hbm, rate_hbm, skip_hbm, out_ref, ahead_ref, behind_ref, skip_ref, mixed, slope, key_ref, value_ref, gate_ref, grad_ref, rate_ref, sems):
    block, width = key_ref.shape
    modes = rate_ref.shape[0]
    halves, groups = modes // SUBLANES, width // LANES
    pairs = ((rate_hbm, rate_ref), (key_hbm, key_ref), (value_hbm, value_ref), (grad_hbm, grad_ref), (gate_hbm, gate_ref), (skip_hbm, skip_ref))
    copies = [pltpu.make_async_copy(source, target, sems.at[at]) for at, (source, target) in enumerate(pairs)]
    for copy in copies:
        copy.start()
    copies[0].wait()
    steps = {}
    for half in range(halves):
        for group in range(groups):
            rate = jnp.exp(rate_ref[half * SUBLANES : (half + 1) * SUBLANES, group * LANES : (group + 1) * LANES])
            steps[half, group] = jnp.exp(-rate)
    copies[1].wait()
    copies[2].wait()
    zero = jnp.zeros((SUBLANES, LANES), jnp.float32)

    def fill(target, one_ref, other_ref):
        for group in range(groups):
            lanes = slice(group * LANES, (group + 1) * LANES)
            for part in range(block // PART):
                at, rows = part * (PART + SUBLANES), slice(part * PART, (part + 1) * PART)
                target[group, at : at + SUBLANES, :] = zero
                product = one_ref[rows, lanes].astype(jnp.float32) * other_ref[rows, lanes].astype(jnp.float32)
                target[group, at + SUBLANES : at + SUBLANES + PART, :] = product
            target[group, block // PART * (PART + SUBLANES) :, :] = zero

    fill(mixed, key_ref, value_ref)
    copies[3].wait()
    copies[4].wait()
    fill(slope, grad_ref, gate_ref)
    copies[5].wait()
    for first in range(0, groups, GROUPS_AT_ONCE):
        held = range(first, first + GROUPS_AT_ONCE)
        keys = [(half, group) for half in range(halves) for group in held]

        def advance(part, carry):
            carry = list(carry)
            for at, (half, group) in enumerate(keys):
                rows = slice(half * SUBLANES, (half + 1) * SUBLANES)
                lanes = slice(group * LANES, (group + 1) * LANES)
                ahead_ref[part, rows, lanes] = carry[at][0]
                behind_ref[block // PART - 1 - part, rows, lanes] = carry[at][4]
            for piece in range(PART // SUBLANES):
                x_tiles = {group: tile_of(mixed, part, piece, group) for group in held}
                z_tiles = {group: tile_of(slope, part, piece, group) for group in held}
                mirror = block // PART - 1 - part, PART // SUBLANES - 1 - piece
                back_tiles = {group: tile_of(slope, *mirror, group) for group in held}
                for inner in range(SUBLANES):
                    x_rows = {group: spread(x_tiles[group], inner) for group in held}
                    z_rows = {group: spread(z_tiles[group], inner) for group in held}
                    back_rows = {group: spread(back_tiles[group], SUBLANES - 1 - inner) for group in held}
                    for at, (half, group) in enumerate(keys):
                        state, timed, plain_sum, timed_sum, back, back_timed = carry[at]
                        step = steps[half, group]
                        moved = step * state
                        timed = step * timed + moved
                        state = moved + x_rows[group]
                        plain_sum = plain_sum + z_rows[group] * state
                        timed_sum = timed_sum + z_rows[group] * timed
                        back_moved = step * back
                        back_timed = step * back_timed + back_moved
                        back = back_moved + back_rows[group]
                        carry[at] = (state, timed, plain_sum, timed_sum, back, back_timed)
            return tuple(carry)

        done = lax.fori_loop(0, block // PART, advance, tuple((zero,) * 6 for _ in keys))
        for at, (half, group) in enumerate(keys):
            state, timed, plain_sum, timed_sum, back, back_timed = done[at]
            step = steps[half, group]
            base = (group * modes + half * SUBLANES) * ROWS_OUT
            skip_part = jnp.sum(mixed[group] * slope[group], axis=0, keepdims=True)
            rows = (
                step * state,
                step * (timed + state),
                back,
                back_timed,
                plain_sum,
                timed_sum,
                jnp.broadcast_to(skip_part, (SUBLANES, LANES)),
            )
            for row, value in enumerate(rows):
                out_ref[pl.ds(base + row, SUBLANES, stride=ROWS_OUT), :] = value


def shifted(value, amount):
    rows = lax.broadcasted_iota(jnp.int32, value.shape, 0)
    moved = pltpu.roll(value, amount % value.shape[0], 0)
    keep = rows >= amount if amount > 0 else rows < value.shape[0] + amount
    return jnp.where(keep, moved, 0.0)


def scan_kernel(block, modes, in_ref, res_ref, rate_ref, out_ref):
    chunk = SUBLANES
    blocks = chunk * SUBLANES
    upper = lax.rem(lax.axis_index("chan"), 2)
    (low_turn, cut), (high_turn, _) = (divmod(-lead % blocks, chunk) for lead in LEADS)
    turn = jnp.where(upper == 1, high_turn, low_turn)
    lead = jnp.where(upper == 1, LEADS[1], LEADS[0])
    seam = lax.broadcasted_iota(jnp.int32, (SUBLANES, LANES), 0) == turn
    place = lax.rem(lax.axis_index("seq") + (blocks - lead), blocks)
    own_mode, own_group = lax.rem(place, modes), lax.div(place, modes)
    rows = lax.broadcasted_iota(jnp.int32, (modes, LANES), 0)

    def own(ref):
        picked = jnp.zeros((modes, LANES), jnp.float32)
        for group in range(ref.shape[1] // LANES):
            mine = rows == jnp.where(own_group == group, own_mode, -1)
            picked = jnp.where(mine, ref[:, group * LANES : (group + 1) * LANES], picked)
        return jnp.broadcast_to(jnp.sum(picked, axis=0, keepdims=True), (SUBLANES, LANES))

    rate = jnp.exp(own(rate_ref))
    unit = jnp.sqrt(2.0 * rate / modes)
    amplitude = own(res_ref) * unit
    power = [jnp.exp(-float(block * v) * rate) for v in range(chunk)]
    decay = power[1]

    def load(v, row):
        return in_ref[pl.ds(v * ROWS_OUT + row, SUBLANES, stride=chunk * ROWS_OUT), :]

    zero = jnp.zeros((SUBLANES, LANES), jnp.float32)
    state, timed, back = zero, zero, zero
    states, timeds, backs = [], [], [None] * chunk
    for v in range(chunk):
        if v == cut:
            state, timed = jnp.where(seam, 0.0, state), jnp.where(seam, 0.0, timed)
        states.append(state)
        timeds.append(timed)
        moved = decay * state
        timed = decay * timed + float(block) * moved + load(v, 1)
        state = moved + load(v, 0)
    for v in reversed(range(chunk)):
        backs[v] = back
        back = decay * back + load(v, 2)
        if v == cut:
            back = jnp.where(seam, 0.0, back)
    state, timed = (pltpu.roll(value, SUBLANES - turn, 0) for value in (state, timed))
    back = pltpu.roll(back, SUBLANES - 1 - turn, 0)
    span = block * chunk
    distance = 1
    while distance < SUBLANES:
        far = jnp.exp(-float(span * distance) * rate)
        older = far * shifted(state, distance)
        timed = timed + far * shifted(timed, distance) + float(span * distance) * older
        state = state + older
        back = back + far * shifted(back, -distance)
        distance *= 2
    state, timed = (pltpu.roll(value, turn + 1, 0) for value in (state, timed))
    back = pltpu.roll(back, turn, 0)
    start_state, start_timed = jnp.where(seam, 0.0, state), jnp.where(seam, 0.0, timed)
    end_back = jnp.where(seam, 0.0, back)
    plain, slow, skip = zero, zero, zero
    for v in range(chunk):
        before, before_timed = (start_state, start_timed) if v >= cut else (state, timed)
        entering = states[v] + power[v] * before
        entering_timed = timeds[v] + power[v] * (before_timed + float(block * v) * before)
        leaving = backs[v] + power[chunk - 1 - v] * (back if v >= cut else end_back)
        slope, slope_timed = load(v, 2), load(v, 3)
        plain = plain + load(v, 4) + slope * entering
        slow = slow + load(v, 5) + slope_timed * entering + slope * entering_timed
        skip = skip + load(v, 6)
        for row, value in ((0, entering), (1, leaving)):
            out_ref[pl.ds(v * ROWS_BACK + row, SUBLANES, stride=chunk * ROWS_BACK), :] = value

    def total(value):
        return jnp.broadcast_to(jnp.sum(value, axis=0, keepdims=True), (SUBLANES, LANES))

    plain, slow, skip = total(plain), total(slow), total(skip)
    raw_res = plain * unit
    raw_log = (0.5 * plain - rate * slow) * amplitude
    for v in range(chunk):
        for row, value in ((2, raw_res), (3, raw_log), (4, skip)):
            out_ref[pl.ds(v * ROWS_BACK + row, SUBLANES, stride=chunk * ROWS_BACK), :] = value


def square_kernel(modes, in_ref, res_ref, log_ref, skip_ref, out_ref):
    groups = res_ref.shape[1] // LANES
    first = lax.broadcasted_iota(jnp.int32, (SUBLANES, LANES), 0) == 0
    total = jnp.zeros((SUBLANES, LANES), jnp.float32)
    for group in range(groups):
        lanes = slice(group * LANES, (group + 1) * LANES)
        for half in range(modes // SUBLANES):
            base = (group * modes + half * SUBLANES) * ROWS_BACK
            for row, ref in ((2, res_ref), (3, log_ref)):
                value = in_ref[pl.ds(base + row, SUBLANES, stride=ROWS_BACK), :]
                ref[half * SUBLANES : (half + 1) * SUBLANES, lanes] = value
                total = total + value * value
        skip = in_ref[pl.ds(group * modes * ROWS_BACK + 4, 1), :]
        skip_ref[:, lanes] = skip
        total = total + jnp.where(first, skip * skip, 0.0)
    out_ref[...] = jnp.broadcast_to(jnp.sum(total, axis=0, keepdims=True), out_ref.shape)


def output_kernel(count, in_ref, squares_ref, raw_res_ref, raw_log_ref, raw_skip_ref, ahead_ref, behind_ref, mixed_ref, slope_ref, key_ref, value_ref, gate_ref, grad_ref, res_ref, rate_ref, skip_ref, out_hbm, gate_hbm, key_hbm, value_hbm, res_hbm, log_hbm, gain_hbm, out_ref, gate_out, key_out, value_out, entering, leaving, taps, res_out, log_out, gain_out, sems, clip_sems):
    block, width = key_ref.shape
    modes = rate_ref.shape[0]
    groups = width // LANES
    parts, halves = block // PART, modes // SUBLANES
    tile = (SUBLANES, LANES)
    zero = jnp.zeros(tile, jnp.float32)
    place = lax.broadcasted_iota(jnp.int32, tile, 0)
    odd, second, fourth = ((place & bit) != 0 for bit in (1, 2, 4))

    def row(ref, at):
        return jnp.broadcast_to(ref[at : at + 1, :], tile)

    squares = jnp.sum(jnp.sum(squares_ref[...], axis=0, keepdims=True), axis=1, keepdims=True)
    factor = CLIP_RMS / jnp.maximum(jnp.sqrt(squares / count), CLIP_RMS)
    copies = []
    for at, (raw, held, target) in enumerate(
        ((raw_res_ref, res_out, res_hbm), (raw_log_ref, log_out, log_hbm), (raw_skip_ref, gain_out, gain_hbm))
    ):
        held[...] = raw[...] * factor
        copies.append(pltpu.make_async_copy(held, target, clip_sems.at[at]))
        copies[-1].start()

    def leave(group, first, *pairs):
        lanes = slice(group * LANES, (group + 1) * LANES)
        for at, (source, target) in enumerate(pairs):
            copies.append(pltpu.make_async_copy(source.at[:, lanes], target.at[:, lanes], sems.at[group, first + at]))
            copies[-1].start()

    for group in range(groups):
        lanes = slice(group * LANES, (group + 1) * LANES)
        mixed, slope = mixed_ref.at[group], slope_ref.at[group]
        powers = []
        for half in range(halves):
            rows = slice(half * SUBLANES, (half + 1) * SUBLANES)
            rate = jnp.exp(rate_ref[rows, lanes])
            amplitude = res_ref[rows, lanes] * jnp.sqrt(2.0 * rate / modes)
            step, leap = jnp.exp(-rate), jnp.exp(-float(PART) * rate)
            square = step * step
            powers.append((amplitude, step, square, square * square, jnp.exp(-float(SUBLANES) * rate)))
            base = (group * modes + half * SUBLANES) * ROWS_BACK
            wave = in_ref[pl.ds(base, SUBLANES, stride=ROWS_BACK), :]
            echo = in_ref[pl.ds(base + 1, SUBLANES, stride=ROWS_BACK), :]
            for part in range(parts):
                mirror = parts - 1 - part
                at, mirrored = part * modes + half * SUBLANES, mirror * modes + half * SUBLANES
                entering[at : at + SUBLANES, :] = amplitude * (step * ahead_ref[part, rows, lanes] + wave)
                leaving[mirrored : mirrored + SUBLANES, :] = amplitude * (behind_ref[mirror, rows, lanes] + echo)
                if part + 1 < parts:
                    wave, echo = wave * leap, echo * leap
        ahead, back = [zero] * (2 * parts), [zero] * (2 * parts)
        near, far = zero, zero
        for mode in range(modes):
            half, inner = divmod(mode, SUBLANES)
            amplitude, step, square, fourth_power, jump = (spread(power, inner) for power in powers[half])
            up = jnp.where(odd, step, 1.0) * jnp.where(second, square, 1.0) * jnp.where(fourth, fourth_power, 1.0)
            down = step * jnp.where(odd, 1.0, step) * jnp.where(second, 1.0, square) * jnp.where(fourth, 1.0, fourth_power)
            tap = amplitude * up
            near, far = near + tap, far + tap * jump
            for part in range(parts):
                wave = row(entering, part * modes + mode) * up
                echo = row(leaving, part * modes + mode) * down
                ahead[2 * part] = ahead[2 * part] + wave
                ahead[2 * part + 1] = ahead[2 * part + 1] + wave * jump
                back[2 * part + 1] = back[2 * part + 1] + echo
                back[2 * part] = back[2 * part] + echo * jump
        taps[0:SUBLANES, :] = near
        taps[SUBLANES:, :] = far
        skip_row = jnp.broadcast_to(skip_ref[:, lanes], tile)
        for shift in range(SUBLANES):
            close, apart = row(taps, shift), row(taps, SUBLANES + shift)
            if shift == 0:
                close = close + skip_row
            for part in range(parts):
                start = part * (PART + SUBLANES) + SUBLANES
                low = mixed[pl.ds(start - shift, SUBLANES), :]
                high = mixed[pl.ds(start + SUBLANES - shift, SUBLANES), :]
                ahead[2 * part] = ahead[2 * part] + close * low
                ahead[2 * part + 1] = ahead[2 * part + 1] + (close * high + apart * low)
        for pair in range(parts):
            rows = slice(pair * PART, (pair + 1) * PART)
            filtered = jnp.concatenate([ahead[2 * pair], ahead[2 * pair + 1]], axis=0)
            out_ref[rows, lanes] = (gate_ref[rows, lanes].astype(jnp.float32) * filtered).astype(jnp.bfloat16)
            gate_out[rows, lanes] = (grad_ref[rows, lanes].astype(jnp.float32) * filtered).astype(jnp.bfloat16)
        leave(group, 0, (out_ref, out_hbm), (gate_out, gate_hbm))
        for shift in range(SUBLANES):
            close, apart = row(taps, shift), row(taps, SUBLANES + shift)
            if shift == 0:
                close = close + skip_row
            for part in range(parts):
                start = part * (PART + SUBLANES) + SUBLANES
                low = slope[pl.ds(start + shift, SUBLANES), :]
                high = slope[pl.ds(start + SUBLANES + shift, SUBLANES), :]
                back[2 * part] = back[2 * part] + (close * low + apart * high)
                back[2 * part + 1] = back[2 * part + 1] + close * high
        for pair in range(parts):
            rows = slice(pair * PART, (pair + 1) * PART)
            mixed_grad = jnp.concatenate([back[2 * pair], back[2 * pair + 1]], axis=0)
            key_out[rows, lanes] = (value_ref[rows, lanes].astype(jnp.float32) * mixed_grad).astype(jnp.bfloat16)
            value_out[rows, lanes] = (key_ref[rows, lanes].astype(jnp.float32) * mixed_grad).astype(jnp.bfloat16)
        leave(group, 2, (key_out, key_hbm), (value_out, value_hbm))
    for copy in copies:
        copy.wait()


def in_hbm(*arrays):
    return tuple(pltpu.with_memory_space_constraint(array, pltpu.HBM) for array in arrays)


def call(kernel, out_shape, *args, scratch=(), space=VMEM, out_space=VMEM):
    multiple = isinstance(out_shape, (tuple, list))
    return pl.pallas_call(
        kernel,
        out_shape=out_shape,
        in_specs=[space] * len(args),
        out_specs=[out_space] * len(out_shape) if multiple else out_space,
        scratch_shapes=list(scratch),
        compiler_params=PARAMS,
    )(*args)


def exchange(rows, axis, groups=None):
    count, lanes = rows.shape
    moved = lax.all_to_all(rows.reshape(count, 1, lanes), axis, 0, 0, axis_index_groups=groups, tiled=True)
    return moved.reshape(count, lanes)


def near_groups(blocks, shards):
    run = blocks // Y_RUN
    groups = []
    for device in range(blocks):
        other = device ^ (2 * run)
        members = [(other if shard % 2 else device) * shards + shard for shard in range(shards)]
        groups.append(members[ROOT_HIGH:] + members[:ROOT_HIGH])
    return groups


def floats(*shape):
    return jax.ShapeDtypeStruct(shape, jnp.float32)


def summarize(key_in, value_in, gate_in, out_grad, log_rate, skip):
    block, width = key_in.shape
    modes = log_rate.shape[0]
    return call(
        summary_kernel,
        (
            floats(modes * (width // LANES) * ROWS_OUT, LANES),
            floats(block // PART, modes, width),
            floats(block // PART, modes, width),
            floats(1, width),
            floats(width // LANES, block // PART * (PART + SUBLANES) + SUBLANES, LANES),
            floats(width // LANES, block // PART * (PART + SUBLANES) + SUBLANES, LANES),
        ),
        *in_hbm(key_in, value_in, gate_in, out_grad, log_rate, skip),
        scratch=[pltpu.VMEM((block, width), jnp.bfloat16)] * 4
        + [pltpu.VMEM((modes, width), jnp.float32)]
        + [pltpu.SemaphoreType.DMA((6,))],
        space=pl.BlockSpec(memory_space=pltpu.HBM),
    )


def finish(states, squares, raw_res, raw_log, raw_skip, ahead, behind, mixed, slope, key_in, value_in, gate_in, out_grad, residue, log_rate, skip_row):
    block, width = key_in.shape
    modes, groups, shards = residue.shape[0], width // LANES, squares.shape[0]
    return call(
        functools.partial(output_kernel, float((2 * modes + 1) * width * shards)),
        (jax.ShapeDtypeStruct((block, width), jnp.bfloat16),) * 4 + (floats(modes, width), floats(modes, width), floats(1, width)),
        states, squares, raw_res, raw_log, raw_skip, ahead, behind, mixed, slope, key_in, value_in, gate_in, out_grad, residue, log_rate, skip_row,
        out_space=pl.BlockSpec(memory_space=pl.ANY),
        scratch=[pltpu.VMEM((block, width), jnp.bfloat16)] * 4
        + [pltpu.VMEM((block // PART * modes, LANES), jnp.float32)] * 2
        + [pltpu.VMEM((PART, LANES), jnp.float32)]
        + [pltpu.VMEM((modes, width), jnp.float32)] * 2
        + [pltpu.VMEM((1, width), jnp.float32), pltpu.SemaphoreType.DMA((groups, 4)), pltpu.SemaphoreType.DMA((3,))],
    )


def per_device(gate_in, key_in, value_in, out_grad, residue, log_rate, skip):
    block, width = gate_in.shape
    modes = residue.shape[0]
    blocks = lax.axis_size("seq")
    shards = lax.axis_size("chan")
    groups = width // LANES
    owners = groups * modes
    assert owners == blocks
    orders = [[(LEADS[shard % 2] + at) % blocks * shards + shard for at in range(blocks)] for shard in range(shards)]
    sent, ahead, behind, skip_row, mixed, slope = summarize(key_in, value_in, gate_in, out_grad, log_rate, skip.reshape(1, width))
    arrived = exchange(sent, ("seq", "chan"), orders)
    reply = call(
        functools.partial(scan_kernel, block, modes),
        floats(blocks * ROWS_BACK, LANES),
        arrived, residue, log_rate,
    )
    states = exchange(reply, ("seq", "chan"), orders)
    raw_res, raw_log, raw_skip, squares = call(
        functools.partial(square_kernel, modes),
        (floats(modes, width), floats(modes, width), floats(1, width), floats(shards, LANES)),
        states,
    )
    squares = exchange(squares, ("seq", "chan"), near_groups(blocks, shards))
    gated_out, gate_grad, key_grad, value_grad, residue_grad, log_rate_grad, skip_grad = finish(
        states, squares, raw_res, raw_log, raw_skip, ahead, behind, mixed, slope, key_in, value_in, gate_in, out_grad, residue, log_rate, skip_row
    )
    return gated_out, gate_grad, key_grad, value_grad, residue_grad, log_rate_grad, skip_grad.reshape(width)


def solution(mesh):
    field, parameter, gain = P("seq", "chan"), P(None, "chan"), P("chan")
    return jax.shard_map(
        per_device,
        mesh=mesh,
        in_specs=(field, field, field, field, parameter, parameter, gain),
        out_specs=(field, field, field, field, parameter, parameter, gain),
        check_vma=False,
    )
```
